32 devices in a mesh: clip: 2 (over y), seq: 4 (over z), tm: 2 (over x), chan: 2 (over core).
Axes of the slice: x: 2, y: 2, z: 4, core: 2. Of those that a mesh axis runs over, the one named last changes fastest.
Arguments:
- latents: bfloat16 [4, 16, 28800], P(('clip', 'tm'), None, 'seq'), parts along dimension 0, may hold values from -6 to 6
- conv_in: bfloat16 [3, 3, 3, 16, 512], P(None, None, None, None, 'chan'), may hold values from -0.3125 to 0.3125
- conv_up: bfloat16 [3, 3, 3, 512, 256], P(None, None, None, None, 'chan'), may hold values from -0.0546875 to 0.0546875
- to_pixels: bfloat16 [256, 12], P('chan'), may hold values from -0.375 to 0.375
- slot_anchor: int32 [4, 3, 16], P(('clip', 'tm'), None, 'seq'), parts along dimension 0, may hold values from 0 to 144, as said below
- slot_count: int32 [4, 4], P(('clip', 'tm'), 'seq'), parts along dimension 0, may hold values from 1 to 4, 8 in all within a row
Outputs:
- pixels: bfloat16 [4, 16, 3, 1, 128], P(('clip', 'tm'), 'seq'), parts along dimension 0
The draws below stay inside these ranges and needn't reach their ends.
There are 2 independent parts, one for each index of `clip`. The reference program is written for one: setup_inputs(seed, part) draws one part's arguments, and reference() takes and returns one part's arrays. A program takes and returns all parts, laid end to end along the dimension named above; an argument that names none is the same for every part. Nothing has to cross between parts.
Inputs may be any that keep to these rules, and one draw needn't show every extreme that they name: `slot_count`: over the devices of one temporal group the counts sum to 2 times the number of devices; the largest count of each group is 4. `slot_anchor`: component 0 is a frame from 0 to 3, component 1 a row from 0 to 43, component 2 a column from 0 to 144; tiles may intersect; slots at or past a device's count are unused.
All inputs are finite; a program needn't handle non-finite values.
Results may differ from the reference program's by a relative error of at most 0.0059.
Values may be sent and summed in bfloat16 or wider, within the bound.
No kernel may reach another device: no remote copies, remote signals or barrier semaphores. Data moves between devices by JAX's collectives and lax.ppermute only.
A program may use at most 64 MiB of HBM per device.

```python
import math
import jax
import jax.numpy as jnp
import numpy as np
from jax import lax

C_LAT = 16
C_MID = 512
C_UP = 256
PIX = 12
H_LAT = 45
W_LAT = 160
FG = 4
TF = 1
TH = 2
TW = 16
TPD = 2
MAXT = 4
GROUPS = 2
SLOTS = 16
GROUP_TOK = 28800
N_SEQ = 4


def draw_slot_anchor(key, part):
    keys = jax.random.split(key, 3)
    frames = jax.random.randint(keys[0], (GROUPS, 1, SLOTS), 0, FG - TF + 1)
    row_part = jax.random.randint(keys[1], (GROUPS, 1, SLOTS), 0, H_LAT - TH + 1)
    col_part = jax.random.randint(keys[2], (GROUPS, 1, SLOTS), 0, W_LAT - TW + 1)
    result = jnp.concatenate([frames, row_part, col_part], axis=1).astype(jnp.int32)
    result = result.at[0, 2, 0].set(W_LAT - TW)
    return result.at[0, 0, 1].set(0)


def levels(key, shape, pieces, least, high):
    loudness, own = 1.0, jax.random.fold_in(key, 6)
    for axis_at, parts in pieces:
        draws = jnp.exp(jax.random.uniform(jax.random.fold_in(own, axis_at), (parts,), jnp.float32, least / len(pieces), high / len(pieces)))
        loudness = loudness * jnp.repeat(draws, shape[axis_at] // parts).reshape([-1 if axis == axis_at else 1 for axis in range(len(shape))])
    return loudness


def split_up(amount, total, most, lean):
    loads = [(1 << 20) // math.isqrt(grade ** lean) + 1 for grade in range(2, amount + 1)]
    spare, holding = total - most - (amount - 1), [1] * (amount - 1)
    while spare > 0:
        movable = [i for i in range(amount - 1) if holding[i] < most]
        pool, left = sum([loads[i] for i in movable]), spare
        for i in movable:
            more = min(most - holding[i], max(1, left * loads[i] // pool), spare)
            holding[i] = holding[i] + more
            spare = spare - more
    return np.array([most] + holding)


def uneven(own_key, amount, total, reach, lean):
    if amount == 2:
        one = jax.random.randint(own_key, (), max(1, total - reach), min(reach, total - 1) + 1)
        return jnp.stack([one, total - one])
    tallies = jnp.asarray(split_up(amount, total, reach, lean), jnp.int32)
    pairs = (amount - 1) // 2
    source_of, receiver = tallies[1:1 + 2 * pairs:2], tallies[2:2 + 2 * pairs:2]
    slack = jnp.minimum(source_of - 1, reach - receiver)
    shifted = jax.random.randint(jax.random.fold_in(own_key, 1), (pairs,), 0, 1 << 20) % (slack + 1)
    tallies = tallies.at[1:1 + 2 * pairs:2].set(source_of - shifted).at[2:2 + 2 * pairs:2].set(receiver + shifted)
    return tallies[jax.random.permutation(jax.random.fold_in(own_key, 2), amount)]


def bell_draw(stream_key, shape, width, bound, shards=(), held_as=jnp.bfloat16):
    drawn = jax.random.normal(stream_key, shape, jnp.float32) * width
    if len(shards) > 0:
        drawn = levels(stream_key, shape, shards, -0.22, 0.18) * drawn
    return jnp.clip(drawn, min=-bound, max=bound).astype(held_as)


def setup_inputs(seed: int = 0, part: int = 0) -> dict:
    key_list = jax.random.split(jax.random.key(seed), 7)
    own_keys = jax.random.split(jax.random.fold_in(key_list[6], part), 7)
    latents = bell_draw(own_keys[0], (GROUPS, C_LAT, GROUP_TOK), 1.0, 6.0, ((0, 2), (2, 4)))
    conv_in = bell_draw(key_list[1], (3, 3, 3, C_LAT, C_MID), (27 * C_LAT) ** -0.5, 0.3125, ((4, 2),))
    conv_up = bell_draw(key_list[2], (3, 3, 3, C_MID, C_UP), (27 * C_MID) ** -0.5, 0.0546875, ((4, 2),))
    to_pixels = bell_draw(key_list[3], (C_UP, PIX), C_UP ** -0.5, 0.375, ((0, 2),))
    slot_anchor = draw_slot_anchor(jax.random.fold_in(jax.random.fold_in(key_list[6], part), 71), part)
    slot_count = jax.vmap(lambda own: uneven(own, N_SEQ, TPD * N_SEQ, MAXT, 2))(jax.random.split(own_keys[5], GROUPS)).reshape((GROUPS, N_SEQ)).astype(jnp.int32)
    return dict(latents=latents, conv_in=conv_in, conv_up=conv_up, to_pixels=to_pixels, slot_anchor=slot_anchor, slot_count=slot_count)


def edge_mask(row_start, col_start, span_h, span_w):
    row_ids = row_start + jnp.arange(span_h, dtype=jnp.int32)
    col_ids = col_start + jnp.arange(span_w, dtype=jnp.int32)
    row_in = (row_ids >= 0) & (row_ids < H_LAT)
    col_in = (col_ids >= 0) & (col_ids < W_LAT)
    return (row_in[:, None] & col_in[None, :]).astype(jnp.float32)


def convolve(volume, kernel, layout):
    return lax.conv_general_dilated(volume, kernel, (1, 1, 1), "VALID", dimension_numbers=(layout, "DHWIO", "NDHWC"), precision=lax.Precision.HIGHEST)


def decode_tile(window, row_start, col_start, kernel_in, kernel_up, to_pixels):
    pre_act = convolve(window[None], kernel_in, "NCDHW")[0]
    edge_keep = edge_mask(row_start - 1, col_start - 1, TH + 2, TW + 2)
    hidden = (jax.nn.silu(pre_act) * edge_keep[None, :, :, None]).astype(jnp.bfloat16)
    hidden = lax.optimization_barrier(hidden).astype(jnp.float32)
    mid_pre = convolve(hidden[None], kernel_up, "NDHWC")[0]
    upper = jax.nn.silu(mid_pre).astype(jnp.bfloat16)
    colors = jnp.dot(upper.reshape(-1, C_UP), to_pixels, preferred_element_type=jnp.float32)
    shaped = colors.reshape(TF, TH, TW, 3, 2, 2).transpose(3, 0, 1, 4, 2, 5).reshape(3, TF, 4 * TH * TW)
    return shaped.astype(jnp.bfloat16)


def reference(latents, conv_in, conv_up, to_pixels, slot_anchor, slot_count):
    kernel_in = conv_in.astype(jnp.float32)
    kernel_up = conv_up.astype(jnp.float32)
    video = latents.reshape(GROUPS, C_LAT, FG, H_LAT, W_LAT).transpose(1, 0, 2, 3, 4)
    video = video.reshape(C_LAT, GROUPS * FG, H_LAT, W_LAT)
    padded = jnp.pad(video, ((0, 0), (4, 0), (2, 2), (2, 2)))
    offsets = jnp.cumsum(slot_count, axis=1) - slot_count
    item_ids = jnp.arange(TPD * N_SEQ, dtype=jnp.int32)
    owners = jnp.sum((offsets[:, None, :] <= item_ids[None, :, None]).astype(jnp.int32), axis=2) - 1
    columns = (owners * MAXT + item_ids[None, :] - jnp.take_along_axis(offsets, owners, axis=1)).astype(jnp.int32)
    group_ids = jnp.broadcast_to(jnp.arange(GROUPS, dtype=jnp.int32)[:, None], columns.shape)
    anchors = jnp.take_along_axis(slot_anchor, jnp.repeat(columns[:, None, :], 3, axis=1), axis=2)
    flat_groups = group_ids.reshape(-1)
    flat_anchors = anchors.transpose(0, 2, 1).reshape(-1, 3).astype(jnp.int32)
    zero_index = jnp.zeros((), jnp.int32)

    def one_item(packed):
        group, anchor = packed
        start = (group * FG + anchor[0]).astype(jnp.int32)
        window = lax.dynamic_slice(padded, (zero_index, start, anchor[1], anchor[2]), (C_LAT, TF + 4, TH + 4, TW + 4))
        return decode_tile(window.astype(jnp.float32), anchor[1], anchor[2], kernel_in, kernel_up, to_pixels)

    decoded = lax.map(one_item, (flat_groups, flat_anchors))
    result = jnp.zeros((GROUPS, SLOTS, 3, TF, 4 * TH * TW), jnp.bfloat16)
    return result.at[flat_groups, columns.reshape(-1)].set(decoded)
```

```python
import functools

import jax
import jax.numpy as jnp
from jax import lax
from jax.experimental import pallas as pl
from jax.experimental.pallas import tpu as pltpu
from jax.sharding import PartitionSpec as P

H_LAT = 45
W_LAT = 160
C_LAT = 16
C_MID = 512
FG = 4
TH = 2
TW = 16
MAXT = 4
ROWS = TH + 4
COLS = TW + 4
LANES = 128
ITEM = LANES // MAXT
TAPS = 3
BF16 = jnp.bfloat16
F32 = jnp.float32
VMEM = pl.BlockSpec(memory_space=pltpu.VMEM)
SMEM = pl.BlockSpec(memory_space=pltpu.SMEM)


def lane_ids(rows):
    return lax.broadcasted_iota(jnp.int32, (rows, LANES), 1)


def silu(v):
    return v * (0.5 * jnp.tanh(0.5 * v) + 0.5)


def cut_windows(n, *refs):
    anchors, (cur_ref, prev_ref), outs, src = refs[:n], refs[n : n + 2], refs[n + 2 : -1], refs[-1]
    shard = cur_ref.shape[1]
    per_frame = n // FG
    part_start = lax.rem(lax.axis_index("seq"), per_frame) * shard
    src[:C_LAT, :shard] = prev_ref[...].astype(F32)
    src[C_LAT:, :shard] = cur_ref[...].astype(F32)
    last_base = (shard - 1) // LANES * LANES
    lane = lane_ids(2 * C_LAT)
    for k in range(n):
        for rho in range(ROWS):
            total = jnp.zeros((2 * C_LAT, LANES), F32)
            for i in range(MAXT):
                col0 = anchors[k][0, 2, i] - 2
                start = (anchors[k][0, 1, i] - 2 + rho) * W_LAT + col0 - part_start
                base = jnp.clip(start // LANES * LANES, 0, last_base)
                base = pl.multiple_of(base, LANES)
                off = start - base
                low = src[:, pl.ds(base, LANES)]
                high = src[:, pl.ds(base + LANES, LANES)]
                both = jnp.where(lane >= off, low, high)
                moved = pltpu.roll(both, (ITEM * i - off) & (LANES - 1), 1)
                cell = lane - ITEM * i
                first = jnp.maximum(jnp.maximum(-col0, -start), 0)
                end = jnp.minimum(jnp.minimum(W_LAT - col0, shard - start), COLS)
                total = jnp.where((cell >= first) & (cell < end), moved, total)
            total = total.astype(BF16)
            outs[k][0, rho] = total[:C_LAT]
            outs[k][1, rho] = total[C_LAT:]


def arrange_weights(own_in, other_in, up, pix, in_t, up_t, pix_t):
    me = lax.axis_index("chan")
    half = own_in.shape[1]
    in_t[pl.ds(pl.multiple_of(me * half, half), half), :] = own_in[...].T
    in_t[pl.ds(pl.multiple_of((1 - me) * half, half), half), :] = other_in[...].T
    outs = up.shape[-1]
    for a in range(TAPS):
        for b in range(TAPS):
            for c in range(TAPS):
                at = (a * TAPS + c) * C_MID
                up_t[b * outs : (b + 1) * outs, at : at + C_MID] = up[a, b, c].T
    row = lax.broadcasted_iota(jnp.int32, (32, 12), 0)
    col = lax.broadcasted_iota(jnp.int32, (32, 12), 1)
    pick = ((row % 8) * 4 + row // 8 == col) & (row % 8 < 3)
    pix_t[...] = lax.dot_general(
        pick.astype(BF16), pix[...], (((1,), (1,)), ((), ())), preferred_element_type=F32
    ).astype(BF16)


def decode(n, *refs):
    anchor, parts, (in_t, up_t, pix_t, out, held, hidden) = refs[0], refs[1 : n + 1], refs[n + 1 :]
    per_frame = n // FG
    me = lax.axis_index("seq")
    for k in range(n):
        held[lax.rem(me + n - k, n)] = parts[k][...]
    lane = lane_ids(C_LAT)
    parity = (lane // TW) % 2
    frames = []
    for j in range(5):
        frames.append([])
        where = []
        for i in range(MAXT):
            at = anchor[0, 0, i] + j
            where.append((at // FG, lax.rem(at, FG) * per_frame))
        for rho in range(ROWS):
            total = jnp.zeros((C_LAT, LANES), F32)
            for i, (late, rank) in enumerate(where):
                piece = held[rank, late, rho].astype(F32)
                for p in range(1, per_frame):
                    piece += held[rank + p, late, rho].astype(F32)
                total = jnp.where(lane // ITEM == i, piece, total)
            frames[j].append(total)

    def shifted(v, by):
        by %= LANES
        return v if by == 0 else pltpu.roll(v, by, 1)

    cells = [
        [
            [
                jnp.where(parity == 0, shifted(frames[j][rho], -dx), shifted(frames[j][rho + 1], TW - dx)).astype(BF16)
                for rho in range(5)
            ]
            for dx in range(5)
        ]
        for j in range(5)
    ]
    one_lane = lane_ids(1)
    item, y, x = one_lane // ITEM, (one_lane // TW) % 2, one_lane % TW

    def per_item(values):
        result = jnp.full((1, LANES), values[0], jnp.int32)
        for i in range(1, MAXT):
            result = jnp.where(item == i, values[i], result)
        return result

    row0 = per_item([anchor[0, 1, i] for i in range(MAXT)]) - 1 + y
    col0 = per_item([anchor[0, 2, i] for i in range(MAXT)]) - 1 + x
    rows = jnp.concatenate([row0, row0 + 2], axis=1)
    cols = jnp.concatenate([col0, col0], axis=1)
    row_keep = (rows >= 0) & (rows < H_LAT)
    for t in range(TAPS):
        for c2 in (0, 2):
            sides = []
            for side in (0, 2):
                sides.append(
                    jnp.concatenate(
                        [cells[t + a][c2 + c][b + side] for a in range(TAPS) for b in range(TAPS) for c in range(TAPS)],
                        axis=0,
                    )
                )
            volume = jnp.concatenate(sides, axis=1)
            pre = jnp.dot(in_t[...], volume, preferred_element_type=F32)
            keep = row_keep & (cols + c2 >= 0) & (cols + c2 < W_LAT)
            hidden[pl.ds((t * TAPS + c2) * C_MID, C_MID), :] = jnp.where(keep, silu(pre), 0.0).astype(BF16)
        left = hidden[pl.ds(t * TAPS * C_MID, C_MID), :].astype(F32)
        right = hidden[pl.ds((t * TAPS + 2) * C_MID, C_MID), :].astype(F32)
        last = lax.broadcasted_iota(jnp.int32, left.shape, 1) % TW == TW - 1
        mid = jnp.where(last, pltpu.roll(right, 1, 1), pltpu.roll(left, 2 * LANES - 1, 1))
        hidden[pl.ds((t * TAPS + 1) * C_MID, C_MID), :] = mid.astype(BF16)
    sums = jnp.dot(up_t[...], hidden[...], preferred_element_type=F32)
    outs = sums.shape[0] // TAPS
    first, mid, last = sums[:outs, :LANES], sums[outs : 2 * outs], sums[2 * outs :, LANES:]
    par = (lane_ids(outs) // TW) % 2
    crossed = jnp.where(
        par == 0, pltpu.roll(mid[:, :LANES], LANES - TW, 1), pltpu.roll(mid[:, LANES:], TW, 1)
    )
    upper = silu(first + last + crossed).astype(BF16)
    out[...] = jnp.dot(pix_t[...], upper, preferred_element_type=F32)


def shuffle(count, own, other, out):
    colors = (own[...] + other[...]).astype(BF16).astype(F32)
    lane = lane_ids(8)
    p, q = (lane // 32) % 2, lane % 2
    for i in range(MAXT):
        source = i * ITEM + (lane // 64) * TW + (lane % 32) // 2
        pixel = jnp.zeros((8, LANES), F32)
        for pq in range(4):
            moved = jnp.take_along_axis(colors[8 * pq : 8 * pq + 8], source, axis=1)
            pixel = jnp.where(2 * p + q == pq, moved, pixel)
        pixel = jnp.where(i < count[0, 0], pixel, 0.0).astype(BF16)
        for e in range(3):
            out[0, i, e] = pixel[e : e + 1]


def rotated(x, axis, by):
    size = lax.axis_size(axis)
    return lax.ppermute(x, axis, [(i, (i + by) % size) for i in range(size)])


def local(latents, conv_in, conv_up, to_pixels, slot_anchor, slot_count):
    n = lax.axis_size("seq")
    current = latents[0]
    shard = current.shape[1]
    in_flat = conv_in.reshape(-1, conv_in.shape[-1])
    anchors = [slot_anchor] + [rotated(slot_anchor, "seq", -k) for k in range(1, n)]
    tm_size = lax.axis_size("tm")
    previous = lax.ppermute(current, "tm", [(i, i + 1) for i in range(tm_size - 1)])
    other_in = rotated(in_flat, "chan", 1)
    outs = conv_up.shape[-1]
    in_t, up_t, pix_t = pl.pallas_call(
        arrange_weights,
        out_shape=(
            jax.ShapeDtypeStruct((C_MID, in_flat.shape[0]), BF16),
            jax.ShapeDtypeStruct((TAPS * outs, TAPS * TAPS * C_MID), BF16),
            jax.ShapeDtypeStruct((32, outs), BF16),
        ),
        in_specs=[VMEM] * 4,
        out_specs=(VMEM,) * 3,
        compiler_params=pltpu.CompilerParams(vmem_limit_bytes=32 << 20),
        name="arrange_weights",
    )(in_flat, other_in, conv_up, to_pixels)
    message = (2, ROWS, C_LAT, LANES)
    padded = (shard - 1) // LANES * LANES + 2 * LANES
    cut = pl.pallas_call(
        functools.partial(cut_windows, n),
        out_shape=[jax.ShapeDtypeStruct(message, BF16)] * n,
        in_specs=[SMEM] * n + [VMEM] * 2,
        out_specs=[VMEM] * n,
        scratch_shapes=[pltpu.VMEM((2 * C_LAT, padded), F32)],
        compiler_params=pltpu.CompilerParams(vmem_limit_bytes=16 << 20),
        name="cut_windows",
    )(*anchors, current, previous)
    parts = [cut[0]] + [rotated(cut[k], "seq", k) for k in range(1, n)]
    colors = pl.pallas_call(
        functools.partial(decode, n),
        out_shape=jax.ShapeDtypeStruct((32, LANES), F32),
        in_specs=[SMEM] + [VMEM] * (n + 3),
        out_specs=VMEM,
        scratch_shapes=[
            pltpu.VMEM((n,) + message, BF16),
            pltpu.VMEM((TAPS * TAPS * C_MID, 2 * LANES), BF16),
        ],
        compiler_params=pltpu.CompilerParams(vmem_limit_bytes=32 << 20),
        name="decode",
    )(slot_anchor, *parts, in_t, up_t, pix_t)
    other = rotated(colors, "chan", 1)
    return pl.pallas_call(
        shuffle,
        out_shape=jax.ShapeDtypeStruct((1, MAXT, 3, 1, LANES), BF16),
        in_specs=[SMEM, VMEM, VMEM],
        out_specs=VMEM,
        name="shuffle",
    )(slot_count, colors, other)


def solution(mesh):
    placed = (
        P(("clip", "tm"), None, "seq"),
        P(None, None, None, None, "chan"),
        P(None, None, None, None, "chan"),
        P("chan", None),
        P(("clip", "tm"), None, "seq"),
        P(("clip", "tm"), "seq"),
    )
    return jax.shard_map(
        local,
        mesh=mesh,
        in_specs=placed,
        out_specs=P(("clip", "tm"), "seq", None, None, None),
        check_vma=False,
    )
```

```python
import functools

import jax
import jax.numpy as jnp
from jax import lax
from jax.experimental import pallas as pl
from jax.experimental.pallas import tpu as pltpu
from jax.sharding import PartitionSpec as P

H_LAT = 45
W_LAT = 160
C_LAT = 16
C_MID = 512
FG = 4
TH = 2
TW = 16
MAXT = 4
ROWS = TH + 4
COLS = TW + 4
LANES = 128
ITEM = LANES // MAXT
TAPS = 3
WIDE = 24
BF16 = jnp.bfloat16
F32 = jnp.float32
VMEM = pl.BlockSpec(memory_space=pltpu.VMEM)
SMEM = pl.BlockSpec(memory_space=pltpu.SMEM)
HBM = pl.BlockSpec(memory_space=pltpu.HBM)
ANY = pl.BlockSpec(memory_space=pl.ANY)


def lane_ids(rows):
    return lax.broadcasted_iota(jnp.int32, (rows, LANES), 1)


def silu(v):
    return v * (0.5 * jnp.tanh(0.5 * v) + 0.5)


def fetched(sources, targets, sems):
    copies = [pltpu.make_async_copy(*pair, sems.at[i]) for i, pair in enumerate(zip(sources, targets))]
    for copy in copies:
        copy.start()
    return copies


def stage(ready, *refs):
    del ready
    sources, (cur_out, *outs, cur, sems) = refs[:5], refs[5:]
    copies = []
    for i, pair in enumerate(zip(sources, (cur, *outs))):
        copies.append(pltpu.make_async_copy(*pair, sems.at[i]))
        copies[i].start()
    copies[0].wait()
    cur_out[:, : cur.shape[1]] = cur[...]
    for copy in copies[1:]:
        copy.wait()


def cut_windows(n, *refs):
    count = n // 2 + 1
    anchors, (cur, prev_ref), outs, prev = refs[:count], refs[count : count + 2], refs[count + 2 : -1], refs[-1]
    shard = prev_ref.shape[1]
    per_frame = n // FG
    part_start = lax.rem(lax.axis_index("seq"), per_frame) * shard
    last_base = (shard - 1) // LANES * LANES
    lane = lane_ids(C_LAT)
    prev[:, :shard] = prev_ref[...]
    for k in range(count):
        for i in range(MAXT):
            row0 = anchors[k][1, 0, i] - 2
            col0 = anchors[k][2, 0, i] - 2
            first = jnp.maximum(-col0, 0)
            end = jnp.minimum(W_LAT - col0, COLS)
            totals = [jnp.zeros((C_LAT, LANES), BF16)] * 2
            for rho in range(ROWS):
                start = (row0 + rho) * W_LAT + col0 - part_start
                base = jnp.clip(start & -LANES, 0, last_base)
                base = pl.multiple_of(base, LANES)
                off = start - base
                from_low = lane >= off
                least = COLS * rho + jnp.maximum(first, -start)
                past = COLS * rho + jnp.minimum(end, shard - start)
                keep = (lane >= least) & (lane < past)
                for half, source in enumerate((prev, cur)):
                    low = source[:, pl.ds(base, LANES)]
                    high = source[:, pl.ds(base + LANES, LANES)]
                    moved = pltpu.roll(jnp.where(from_low, low, high), (COLS * rho - off) & (LANES - 1), 1)
                    totals[half] = jnp.where(keep, moved, totals[half])
            for half in range(2):
                outs[k][half, i] = totals[half]


def decode(n, *refs):
    anchor, count, parts = refs[0], refs[1], refs[2 : n + 2]
    own_in, other_in, own_pix, other_pix, own_up, other_up, out, held, hidden, lined = refs[n + 2 :]
    per_frame = n // FG
    me = lax.axis_index("seq")
    core = lax.axis_index("chan")
    held[me] = parts[0][...]
    for k in range(1, n // 2):
        by = jnp.where(core == 0, k, n - k)
        held[lax.rem(me + n - by, n)] = parts[2 * k - 1][...]
        held[lax.rem(me + by, n)] = parts[2 * k][...]
    held[lax.rem(me + n // 2, n)] = parts[n - 1][...]
    lane = lane_ids(C_LAT)

    moved = []
    for j in range(5):
        where = []
        for i in range(MAXT):
            at = anchor[0, 0, i] + j
            where.append((at // FG, lax.rem(at, FG) * per_frame))
        moved.append([])
        pieces = []
        for i, (late, rank) in enumerate(where):
            piece = held[rank, late, i]
            for p in range(1, per_frame):
                piece += held[rank + p, late, i]
            pieces.append(piece)
        for rho in range(ROWS):
            total = None
            for i, piece in enumerate(pieces):
                by = (ITEM * i - COLS * rho) % LANES
                piece = pltpu.roll(piece, by, 1) if by else piece
                total = piece if i == 0 else jnp.where(lane >= ITEM * i, piece, total)
            moved[j].append([total] + [pltpu.roll(total, LANES - c, 1) for c in range(1, TAPS)])

    x = lax.broadcasted_iota(jnp.int32, (WIDE, LANES), 0)
    quarter = C_MID // 4
    for t in range(TAPS):
        cells = jnp.concatenate(
            [
                jnp.concatenate(
                    [moved[t + a][r + b][c] for a in range(TAPS) for b in range(TAPS) for c in range(TAPS)], axis=0
                )
                for r in range(TH + 2)
            ],
            axis=1,
        ).T
        for weights, first in ((own_in, core), (other_in, 1 - core)):
            pre = jnp.dot(cells, weights[...], preferred_element_type=F32)
            for r in range(TH + 2):
                for i in range(MAXT):
                    row = anchor[1, 0, i] - 1 + r
                    col = anchor[2, 0, i] - 1 + x
                    width = jnp.where((row >= 0) & (row < H_LAT), W_LAT, 0)
                    at = (r * MAXT + i) * ITEM
                    value = silu(pre[at : at + WIDE])
                    for q in range(2):
                        hidden[t, r * MAXT + i, 2 * first + q] = jnp.where(
                            (col >= 0) & (col < width), value[:, q * quarter : (q + 1) * quarter], 0.0
                        )
        for c in range(TAPS):
            for ri in range((TH + 2) * MAXT):
                for q in range(4):
                    lined[t * TAPS + c, ri * TW : (ri + 1) * TW, q * quarter : (q + 1) * quarter] = hidden[
                        t, ri, q, c : c + TW
                    ].astype(BF16)
    outs = own_up.shape[-1]
    span = MAXT * TW
    total = jnp.zeros((TH * span, 2 * outs), F32)
    for a in range(TAPS):
        for c in range(TAPS):
            for b in range(TAPS):
                weights = jnp.concatenate([own_up[a, b, c], other_up[a, b, c]], axis=1)
                rows = lined[a * TAPS + c, b * span : (b + TH) * span]
                total += jnp.dot(rows, weights, preferred_element_type=F32)
    upper = silu(total).astype(BF16)
    row = lax.broadcasted_iota(jnp.int32, (32, 12), 0)
    col = lax.broadcasted_iota(jnp.int32, (32, 12), 1)
    pick = ((row % 8) * 4 + row // 8 == col) & (row % 8 < 3)
    pix = jnp.concatenate([own_pix[...], other_pix[...]], axis=1)
    pix = jnp.dot(pick.astype(BF16), pix, preferred_element_type=F32).astype(BF16)
    colors = lax.dot_general(pix, upper, (((1,), (1,)), ((), ())), preferred_element_type=F32)
    colors = colors.astype(BF16).astype(F32)
    lane = lane_ids(8)
    p, q = (lane // 32) % 2, lane % 2
    for i in range(MAXT):
        source = (lane // 64) * span + i * TW + (lane % 32) // 2
        pixel = jnp.zeros((8, LANES), F32)
        for pq in range(4):
            found = jnp.take_along_axis(colors[8 * pq : 8 * pq + 8], source, axis=1)
            pixel = jnp.where(2 * p + q == pq, found, pixel)
        pixel = jnp.where(i < count[0, 0], pixel, 0.0).astype(BF16)
        for e in range(3):
            out[0, e, 0, i : i + 1] = pixel[e : e + 1]


def in_hbm(x):
    return pltpu.with_memory_space_constraint(x, pltpu.HBM)


def swapped(x):
    return lax.ppermute(x, "chan", [(0, 1), (1, 0)])


def spread(x, by):
    size = lax.axis_size("seq")
    pairs = []
    for at in range(size):
        pairs.append((2 * at, 2 * ((at + by) % size)))
        pairs.append((2 * at + 1, 2 * ((at - by) % size) + 1))
    return lax.ppermute(x, ("seq", "chan"), pairs)


def local(latents, conv_in, conv_up, to_pixels, slot_anchor, slot_count):
    n = lax.axis_size("seq")
    current = latents[0]
    shard = current.shape[1]
    anchor = slot_anchor.transpose(1, 0, 2)
    in_flat = conv_in.reshape(-1, conv_in.shape[-1])
    pix = to_pixels.T
    anchors = [spread(anchor, -k) for k in range(1, n // 2 + 1)]
    tm_size = lax.axis_size("tm")
    previous = lax.ppermute(current, "tm", [(i, i + 1) for i in range(tm_size - 1)])
    other_in, other_pix, other_up = swapped(in_flat), swapped(pix), swapped(conv_up)
    padded = (shard - 1) // LANES * LANES + 2 * LANES
    own = (anchor, in_flat, pix, conv_up)
    cur_pad, anchor, own_in, own_pix, own_up = pl.pallas_call(
        stage,
        out_shape=[jax.ShapeDtypeStruct((C_LAT, padded), BF16)] + [jax.ShapeDtypeStruct(x.shape, x.dtype) for x in own],
        in_specs=[ANY] + [HBM] * 5,
        out_specs=[VMEM] * 5,
        scratch_shapes=[pltpu.VMEM(current.shape, BF16), pltpu.SemaphoreType.DMA((5,))],
        compiler_params=pltpu.CompilerParams(vmem_limit_bytes=8 << 20),
        cost_estimate=pl.CostEstimate(flops=1, bytes_accessed=1, transcendentals=0),
        name="stage",
    )(anchors[-1], *map(in_hbm, (current, *own)))
    message = jax.ShapeDtypeStruct((2, MAXT, C_LAT, LANES), BF16)
    cut = pl.pallas_call(
        functools.partial(cut_windows, n),
        out_shape=[message] * (n // 2 + 1),
        in_specs=[SMEM] * (n // 2 + 1) + [VMEM] * 2,
        out_specs=[VMEM] * (n // 2 + 1),
        scratch_shapes=[pltpu.VMEM((C_LAT, padded), BF16)],
        compiler_params=pltpu.CompilerParams(vmem_limit_bytes=4 << 20),
        name="cut_windows",
    )(anchor, *anchors, cur_pad, previous)
    parts = [cut[0]]
    for k in range(1, n // 2):
        arrived = spread(cut[k], k)
        parts += [arrived, swapped(arrived)]
    parts.append(spread(cut[n // 2], n // 2))
    pixels = pl.pallas_call(
        functools.partial(decode, n),
        out_shape=jax.ShapeDtypeStruct((1, 3, 1, MAXT, LANES), BF16),
        in_specs=[SMEM, SMEM] + [VMEM] * (n + 6),
        out_specs=VMEM,
        scratch_shapes=[
            pltpu.VMEM((n,) + message.shape, BF16),
            pltpu.VMEM((TAPS, (TH + 2) * MAXT, 4, WIDE, C_MID // 4), F32),
            pltpu.VMEM((TAPS * TAPS, (TH + 2) * MAXT * TW, C_MID), BF16),
        ],
        compiler_params=pltpu.CompilerParams(vmem_limit_bytes=32 << 20),
        name="decode",
    )(anchor, slot_count, *parts, own_in, other_in, own_pix, other_pix, own_up, other_up)
    return pixels.transpose(0, 3, 1, 2, 4)


def solution(mesh):
    placed = (
        P(("clip", "tm"), None, "seq"),
        P(None, None, None, None, "chan"),
        P(None, None, None, None, "chan"),
        P("chan", None),
        P(("clip", "tm"), None, "seq"),
        P(("clip", "tm"), "seq"),
    )
    return jax.shard_map(
        local,
        mesh=mesh,
        in_specs=placed,
        out_specs=P(("clip", "tm"), "seq", None, None, None),
        check_vma=False,
    )
```

```python
import functools

import jax
import jax.numpy as jnp
from jax import lax
from jax.experimental import pallas as pl
from jax.experimental.pallas import tpu as pltpu
from jax.sharding import PartitionSpec as P

H_LAT = 45
W_LAT = 160
C_LAT = 16
C_MID = 512
FG = 4
TH = 2
TW = 16
MAXT = 4
ROWS = TH + 4
COLS = TW + 4
LANES = 128
TAPS = 3
WIDE = 24
ROOM = 2 * MAXT
BF16 = jnp.bfloat16
F32 = jnp.float32
VMEM = pl.BlockSpec(memory_space=pltpu.VMEM)
SMEM = pl.BlockSpec(memory_space=pltpu.SMEM)
HBM = pl.BlockSpec(memory_space=pltpu.HBM)
ANY = pl.BlockSpec(memory_space=pl.ANY)


def lane_ids(rows):
    return lax.broadcasted_iota(jnp.int32, (rows, LANES), 1)


def silu(v):
    return v * (0.5 * jnp.tanh(0.5 * v) + 0.5)


def fetched(sources, targets, sems):
    copies = [pltpu.make_async_copy(*pair, sems.at[i]) for i, pair in enumerate(zip(sources, targets))]
    for copy in copies:
        copy.start()
    return copies


def stage(ready, *refs):
    del ready
    (count, *sources), (cur_out, meta, *outs, cur, anchor, sems) = refs[:6], refs[6:]
    copies = []
    for i, pair in enumerate(zip(sources, (cur, anchor, *outs))):
        copies.append(pltpu.make_async_copy(*pair, sems.at[i]))
        copies[i].start()
    copies[0].wait()
    cur_out[:, : cur.shape[1]] = cur[...]
    copies[1].wait()
    meta[:TAPS] = anchor[...]
    meta[TAPS] = jnp.full(meta.shape[1:], count[0, 0], jnp.int32)
    for copy in copies[2:]:
        copy.wait()


def cut_windows(n, *refs):
    count = n // 2 + 1
    anchors, (cur, prev_ref, pix), outs, prev = refs[:count], refs[count : count + 3], refs[count + 3 : -1], refs[-1]
    shard = prev_ref.shape[1]
    per_frame = n // FG
    part_start = lax.rem(lax.axis_index("seq"), per_frame) * shard
    last_base = (shard - 1) // LANES * LANES
    lane = lane_ids(C_LAT)
    prev[:, :shard] = prev_ref[...]
    for k in range(count):
        anchor = anchors[k][...]
        for i in range(MAXT):
            row0 = anchor[1, 0, i] - 2
            col0 = anchor[2, 0, i] - 2
            first = jnp.maximum(-col0, 0)
            end = jnp.minimum(W_LAT - col0, COLS)
            totals = [jnp.zeros((C_LAT, LANES), BF16)] * 2
            for rho in range(ROWS):
                start = (row0 + rho) * W_LAT + col0 - part_start
                base = jnp.clip(start & -LANES, 0, last_base)
                base = pl.multiple_of(base, LANES)
                off = start - base
                from_low = lane >= off
                least = COLS * rho + jnp.maximum(first, -start)
                past = COLS * rho + jnp.minimum(end, shard - start)
                keep = (lane >= least) & (lane < past)
                for half, source in enumerate((prev, cur)):
                    low = source[:, pl.ds(base, LANES)]
                    high = source[:, pl.ds(base + LANES, LANES)]
                    moved = pltpu.roll(jnp.where(from_low, low, high), (COLS * rho - off) & (LANES - 1), 1)
                    totals[half] = jnp.where(keep, moved, totals[half])
            for half in range(2):
                outs[k][half * MAXT + i] = totals[half]
    for out in outs[1:]:
        out[ROOM] = jnp.concatenate([pix[...], jnp.zeros((C_LAT - pix.shape[0], LANES), BF16)], axis=0)


def decode(n, *refs):
    anchor, parts = refs[0][...], refs[1 : n + 1]
    own_in, other_in, own_pix, own_up, other_up, out, held, *scratch = refs[n + 1 :]
    hiddens, lineds = scratch[:TAPS], scratch[TAPS:]
    per_frame = n // FG
    me = lax.axis_index("seq")
    core = lax.axis_index("chan")
    held[me] = parts[0][...]
    for k in range(1, n // 2):
        by = jnp.where(core == 0, k, n - k)
        held[lax.rem(me + n - by, n)] = parts[2 * k - 1][:ROOM]
        held[lax.rem(me + by, n)] = parts[2 * k][:ROOM]
    held[lax.rem(me + n // 2, n)] = parts[n - 1][:ROOM]
    lane = lane_ids(C_LAT)

    def frame(j):
        pieces = []
        for i in range(MAXT):
            at = jnp.clip(anchor[0, 0, i], 0, FG - 1) + j
            late, rank = at // FG, lax.rem(at, FG) * per_frame
            piece = held[rank, late * MAXT + i]
            for p in range(1, per_frame):
                piece += held[rank + p, late * MAXT + i]
            pieces.append(piece)
        result = []
        for rho in range(ROWS):
            total = None
            for i, piece in enumerate(pieces):
                by = (WIDE * i - COLS * rho) % LANES
                piece = pltpu.roll(piece, by, 1) if by else piece
                total = piece if i == 0 else jnp.where(lane >= WIDE * i, piece, total)
            result.append([total] + [pltpu.roll(total, LANES - c, 1) for c in range(1, TAPS)])
        return result

    def turned(pieces):
        zeros = [jnp.zeros((C_LAT, LANES), BF16)] * (LANES // C_LAT - len(pieces))
        return jnp.concatenate(pieces + zeros, axis=0).T[: MAXT * WIDE]

    taps = [(b, c) for b in range(TAPS) for c in range(TAPS)]
    spots = range(TH + 2)
    frames = [frame(j) for j in range(TAPS + 2)]
    cells = [
        jnp.concatenate([turned([frames[j][r + b][c] for b, c in taps[:-1]]) for r in spots], axis=0)
        for j in range(TAPS + 2)
    ]
    tail = jnp.concatenate([turned([frames[j][r + 2][2] for j in range(TAPS + 2)]) for r in spots], axis=0)
    x = lax.broadcasted_iota(jnp.int32, (WIDE, LANES), 0)
    quarter, half = C_MID // 4, C_MID // 2
    for t in range(TAPS):
        volume = jnp.concatenate([*cells[t : t + TAPS], tail], axis=1)
        hidden, lined = hiddens[t], lineds[t]
        for first, weights in enumerate((own_in, other_in)):
            per_tap = len(taps) * C_LAT
            kernel = [weights[a * per_tap : a * per_tap + LANES] for a in range(TAPS)]
            for j in range(LANES // C_LAT):
                a = j - t
                ends = weights[a * per_tap + LANES : (a + 1) * per_tap] if 0 <= a < TAPS else None
                kernel.append(jnp.zeros((C_LAT, half), BF16) if ends is None else ends)
            pre = jnp.dot(volume, jnp.concatenate(kernel, axis=0), preferred_element_type=F32)
            for r in spots:
                for i in range(MAXT):
                    row = anchor[1, 0, i] - 1 + r
                    col = anchor[2, 0, i] - 1 + x
                    width = jnp.where((row >= 0) & (row < H_LAT), W_LAT, 0)
                    at = (r * MAXT + i) * WIDE
                    value = silu(pre[at : at + WIDE])
                    for q in range(2):
                        hidden[r * MAXT + i, 2 * first + q] = jnp.where(
                            (col >= 0) & (col < width), value[:, q * quarter : (q + 1) * quarter], 0.0
                        )
        for c in range(TAPS):
            for ri in range((TH + 2) * MAXT):
                for q in range(4):
                    lined[c, ri * TW : (ri + 1) * TW, q * quarter : (q + 1) * quarter] = hidden[
                        ri, q, c : c + TW
                    ].astype(BF16)
    outs = own_up.shape[-1]
    span = MAXT * TW
    total = jnp.zeros((TH * span, 2 * outs), F32)
    for a in range(TAPS):
        for c in range(TAPS):
            for b in range(TAPS):
                rows = lineds[a][c, b * span : (b + TH) * span]
                for first in range(2):
                    here = pl.ds(pl.multiple_of((first ^ core) * half, half), half)
                    weights = jnp.concatenate([own_up[a, b, c, here], other_up[a, b, c, here]], axis=1)
                    total += jnp.dot(rows[:, first * half : (first + 1) * half], weights, preferred_element_type=F32)
    upper = silu(total).astype(BF16)
    row = lax.broadcasted_iota(jnp.int32, (32, 12), 0)
    col = lax.broadcasted_iota(jnp.int32, (32, 12), 1)
    pick = ((row % 8) * 4 + row // 8 == col) & (row % 8 < 3)
    pix = jnp.concatenate([own_pix[...], parts[2][ROOM, : own_pix.shape[0]]], axis=1)
    pix = jnp.dot(pick.astype(BF16), pix, preferred_element_type=F32).astype(BF16)
    colors = lax.dot_general(pix, upper, (((1,), (1,)), ((), ())), preferred_element_type=F32)
    colors = colors.astype(BF16).astype(F32)
    lane = lane_ids(8)
    p, q = (lane // 32) % 2, lane % 2
    for i in range(MAXT):
        source = (lane // 64) * span + i * TW + (lane % 32) // 2
        pixel = jnp.zeros((8, LANES), F32)
        for pq in range(4):
            found = jnp.take_along_axis(colors[8 * pq : 8 * pq + 8], source, axis=1)
            pixel = jnp.where(2 * p + q == pq, found, pixel)
        pixel = jnp.where(i < anchor[TAPS, 0, 0], pixel, 0.0).astype(BF16)
        for e in range(3):
            out[0, e, 0, i : i + 1] = pixel[e : e + 1]


def in_hbm(x):
    return pltpu.with_memory_space_constraint(x, pltpu.HBM)


def swapped(x):
    return lax.ppermute(x, "chan", [(0, 1), (1, 0)])


def spread(x, by):
    size = lax.axis_size("seq")
    pairs = []
    for at in range(size):
        pairs.append((2 * at, 2 * ((at + by) % size)))
        pairs.append((2 * at + 1, 2 * ((at - by) % size) + 1))
    return lax.ppermute(x, ("seq", "chan"), pairs)


def local(latents, conv_in, conv_up, to_pixels, slot_anchor, slot_count):
    n = lax.axis_size("seq")
    current = latents[0]
    shard = current.shape[1]
    anchor = slot_anchor.transpose(1, 0, 2)
    in_flat = conv_in.reshape(-1, conv_in.shape[-1])
    pix = to_pixels.T
    anchors = [spread(anchor, -k) for k in range(1, n // 2 + 1)]
    tm_size = lax.axis_size("tm")
    previous = lax.ppermute(current, "tm", [(i, i + 1) for i in range(tm_size - 1)])
    other_in, other_up = swapped(in_flat), swapped(conv_up)
    padded = (shard - 1) // LANES * LANES + 2 * LANES
    own = (in_flat, pix, conv_up)
    cur_pad, meta, own_in, own_pix, own_up = pl.pallas_call(
        stage,
        out_shape=[
            jax.ShapeDtypeStruct((C_LAT, padded), BF16),
            jax.ShapeDtypeStruct((TAPS + 1, *anchor.shape[1:]), jnp.int32),
            *(jax.ShapeDtypeStruct(x.shape, BF16) for x in own),
        ],
        in_specs=[ANY, SMEM] + [HBM] * 5,
        out_specs=[VMEM] * 5,
        scratch_shapes=[
            pltpu.VMEM(current.shape, BF16),
            pltpu.VMEM(anchor.shape, jnp.int32),
            pltpu.SemaphoreType.DMA((5,)),
        ],
        compiler_params=pltpu.CompilerParams(vmem_limit_bytes=8 << 20),
        cost_estimate=pl.CostEstimate(flops=1, bytes_accessed=1, transcendentals=0),
        name="stage",
    )(anchors[-1], slot_count, *map(in_hbm, (current, anchor, *own)))
    message = jax.ShapeDtypeStruct((ROOM, C_LAT, LANES), BF16)
    extended = jax.ShapeDtypeStruct((ROOM + 1, C_LAT, LANES), BF16)
    cut = pl.pallas_call(
        functools.partial(cut_windows, n),
        out_shape=[message] + [extended] * (n // 2),
        in_specs=[VMEM] * (n // 2 + 4),
        out_specs=[VMEM] * (n // 2 + 1),
        scratch_shapes=[pltpu.VMEM((C_LAT, padded), BF16)],
        compiler_params=pltpu.CompilerParams(vmem_limit_bytes=4 << 20),
        name="cut_windows",
    )(meta, *anchors, cur_pad, previous, own_pix)
    parts = [cut[0]]
    for k in range(1, n // 2):
        arrived = spread(cut[k], k)
        parts += [arrived, swapped(arrived)]
    parts.append(spread(cut[n // 2], n // 2))
    pixels = pl.pallas_call(
        functools.partial(decode, n),
        out_shape=jax.ShapeDtypeStruct((1, 3, 1, MAXT, LANES), BF16),
        in_specs=[VMEM] * (n + 6),
        out_specs=VMEM,
        scratch_shapes=[
            pltpu.VMEM((n,) + message.shape, BF16),
        ]
        + [pltpu.VMEM(((TH + 2) * MAXT, 4, WIDE, C_MID // 4), F32)] * TAPS
        + [pltpu.VMEM((TAPS, (TH + 2) * MAXT * TW, C_MID), BF16)] * TAPS,
        compiler_params=pltpu.CompilerParams(vmem_limit_bytes=32 << 20),
        name="decode",
    )(meta, *parts, own_in, other_in, own_pix, own_up, other_up)
    return pixels.transpose(0, 3, 1, 2, 4)


def solution(mesh):
    placed = (
        P(("clip", "tm"), None, "seq"),
        P(None, None, None, None, "chan"),
        P(None, None, None, None, "chan"),
        P("chan", None),
        P(("clip", "tm"), None, "seq"),
        P(("clip", "tm"), "seq"),
    )
    return jax.shard_map(
        local,
        mesh=mesh,
        in_specs=placed,
        out_specs=P(("clip", "tm"), "seq", None, None, None),
        check_vma=False,
    )
```

```python
import functools

import jax
import jax.numpy as jnp
from jax import lax
from jax.experimental import pallas as pl
from jax.experimental.pallas import tpu as pltpu
from jax.sharding import PartitionSpec as P

H_LAT = 45
W_LAT = 160
C_LAT = 16
C_MID = 512
FG = 4
TH = 2
TW = 16
MAXT = 4
ROWS = TH + 4
COLS = TW + 4
LANES = 128
TAPS = 3
WIDE = 24
ROOM = 2 * MAXT
BF16 = jnp.bfloat16
F32 = jnp.float32
VMEM = pl.BlockSpec(memory_space=pltpu.VMEM)
SMEM = pl.BlockSpec(memory_space=pltpu.SMEM)
HBM = pl.BlockSpec(memory_space=pltpu.HBM)
ANY = pl.BlockSpec(memory_space=pl.ANY)


def lane_ids(rows):
    return lax.broadcasted_iota(jnp.int32, (rows, LANES), 1)


def silu(v):
    return v * (0.5 * jnp.tanh(0.5 * v) + 0.5)


def fetched(sources, targets, sems):
    copies = [pltpu.make_async_copy(*pair, sems.at[i]) for i, pair in enumerate(zip(sources, targets))]
    for copy in copies:
        copy.start()
    return copies


def stage(*refs):
    sources, (cur_out, *outs, cur, sems) = refs[:5], refs[5:]
    copies = []
    for i, pair in enumerate(zip(sources, (cur, *outs))):
        copies.append(pltpu.make_async_copy(*pair, sems.at[i]))
        copies[i].start()
    copies[0].wait()
    cur_out[:, : cur.shape[1]] = cur[...]
    for copy in copies[1:]:
        copy.wait()


def cut_windows(n, *refs):
    count = (len(refs) - 4) // 2
    anchors, (cur, prev_ref, pix), outs, prev = refs[:count], refs[count : count + 3], refs[count + 3 : -1], refs[-1]
    shard = prev_ref.shape[1]
    per_frame = n // FG
    part_start = lax.rem(lax.axis_index("seq"), per_frame) * shard
    last_base = (shard - 1) // LANES * LANES
    lane = lane_ids(C_LAT)
    prev[:, :shard] = prev_ref[...]
    for k in range(count):
        anchor = anchors[k][...]
        for i in range(MAXT):
            row0 = anchor[1, 0, i] - 2
            col0 = anchor[2, 0, i] - 2
            first = jnp.maximum(-col0, 0)
            end = jnp.minimum(W_LAT - col0, COLS)
            totals = [jnp.zeros((C_LAT, LANES), BF16)] * 2
            for rho in range(ROWS):
                start = (row0 + rho) * W_LAT + col0 - part_start
                base = jnp.clip(start & -LANES, 0, last_base)
                base = pl.multiple_of(base, LANES)
                off = start - base
                from_low = lane >= off
                least = COLS * rho + jnp.maximum(first, -start)
                past = COLS * rho + jnp.minimum(end, shard - start)
                keep = (lane >= least) & (lane < past)
                for half, source in enumerate((prev, cur)):
                    low = source[:, pl.ds(base, LANES)]
                    high = source[:, pl.ds(base + LANES, LANES)]
                    moved = pltpu.roll(jnp.where(from_low, low, high), (COLS * rho - off) & (LANES - 1), 1)
                    totals[half] = jnp.where(keep, moved, totals[half])
            for half in range(2):
                outs[k][half * MAXT + i] = totals[half]
    for out in outs if outs[0].shape[0] > ROOM else ():
        out[ROOM] = jnp.concatenate([pix[...], jnp.zeros((C_LAT - pix.shape[0], LANES), BF16)], axis=0)


def decode(n, *refs):
    count, anchor, parts = refs[0], refs[1][...], refs[2 : n + 2]
    own_in, other_in, own_pix, own_up, other_up, out, held, *scratch = refs[n + 2 :]
    hiddens, lineds = scratch[:TAPS], scratch[TAPS:]
    per_frame = n // FG
    me = lax.axis_index("seq")
    core = lax.axis_index("chan")
    held[me] = parts[0][...]
    for k in range(1, n // 2):
        held[me ^ (2 * k - 1 + core)] = parts[2 * k - 1][:ROOM]
        held[me ^ (2 * k - core)] = parts[2 * k][:ROOM]
    held[me ^ (n - 1)] = parts[n - 1][:ROOM]
    lane = lane_ids(C_LAT)

    def frame(j):
        pieces = []
        for i in range(MAXT):
            at = jnp.clip(anchor[0, 0, i], 0, FG - 1) + j
            late, rank = at // FG, lax.rem(at, FG) * per_frame
            piece = held[rank, late * MAXT + i]
            for p in range(1, per_frame):
                piece += held[rank + p, late * MAXT + i]
            pieces.append(piece)
        result = []
        for rho in range(ROWS):
            total = None
            for i, piece in enumerate(pieces):
                by = (WIDE * i - COLS * rho) % LANES
                piece = pltpu.roll(piece, by, 1) if by else piece
                total = piece if i == 0 else jnp.where(lane >= WIDE * i, piece, total)
            result.append([total] + [pltpu.roll(total, LANES - c, 1) for c in range(1, TAPS)])
        return result

    def turned(pieces):
        zeros = [jnp.zeros((C_LAT, LANES), BF16)] * (LANES // C_LAT - len(pieces))
        return jnp.concatenate(pieces + zeros, axis=0).T[: MAXT * WIDE]

    taps = [(b, c) for b in range(TAPS) for c in range(TAPS)]
    spots = range(TH + 2)
    frames = [frame(j) for j in range(TAPS + 2)]
    cells = [
        jnp.concatenate([turned([frames[j][r + b][c] for b, c in taps[:-1]]) for r in spots], axis=0)
        for j in range(TAPS + 2)
    ]
    tail = jnp.concatenate([turned([frames[j][r + 2][2] for j in range(TAPS + 2)]) for r in spots], axis=0)
    x = lax.broadcasted_iota(jnp.int32, (WIDE, LANES), 0)
    quarter, half = C_MID // 4, C_MID // 2
    for t in range(TAPS):
        volume = jnp.concatenate([*cells[t : t + TAPS], tail], axis=1)
        hidden, lined = hiddens[t], lineds[t]
        for first, weights in enumerate((own_in, other_in)):
            per_tap = len(taps) * C_LAT
            kernel = [weights[a * per_tap : a * per_tap + LANES] for a in range(TAPS)]
            for j in range(LANES // C_LAT):
                a = j - t
                ends = weights[a * per_tap + LANES : (a + 1) * per_tap] if 0 <= a < TAPS else None
                kernel.append(jnp.zeros((C_LAT, half), BF16) if ends is None else ends)
            pre = jnp.dot(volume, jnp.concatenate(kernel, axis=0), preferred_element_type=F32)
            for r in spots:
                for i in range(MAXT):
                    row = anchor[1, 0, i] - 1 + r
                    col = anchor[2, 0, i] - 1 + x
                    width = jnp.where((row >= 0) & (row < H_LAT), W_LAT, 0)
                    at = (r * MAXT + i) * WIDE
                    value = silu(pre[at : at + WIDE])
                    for q in range(2):
                        hidden[r * MAXT + i, 2 * first + q] = jnp.where(
                            (col >= 0) & (col < width), value[:, q * quarter : (q + 1) * quarter], 0.0
                        )
        for c in range(TAPS):
            for ri in range((TH + 2) * MAXT):
                for q in range(4):
                    lined[c, ri * TW : (ri + 1) * TW, q * quarter : (q + 1) * quarter] = hidden[
                        ri, q, c : c + TW
                    ].astype(BF16)
    outs = own_up.shape[-1]
    span = MAXT * TW
    total = jnp.zeros((TH * span, 2 * outs), F32)
    for a in range(TAPS):
        for c in range(TAPS):
            for b in range(TAPS):
                rows = lineds[a][c, b * span : (b + TH) * span]
                for first in range(2):
                    here = pl.ds(pl.multiple_of((first ^ core) * half, half), half)
                    weights = jnp.concatenate([own_up[a, b, c, here], other_up[a, b, c, here]], axis=1)
                    total += jnp.dot(rows[:, first * half : (first + 1) * half], weights, preferred_element_type=F32)
    upper = silu(total).astype(BF16)
    row = lax.broadcasted_iota(jnp.int32, (32, 12), 0)
    col = lax.broadcasted_iota(jnp.int32, (32, 12), 1)
    pick = ((row % 8) * 4 + row // 8 == col) & (row % 8 < 3)
    pix = jnp.concatenate([own_pix[...], parts[2][ROOM, : own_pix.shape[0]]], axis=1)
    pix = jnp.dot(pick.astype(BF16), pix, preferred_element_type=F32).astype(BF16)
    colors = lax.dot_general(pix, upper, (((1,), (1,)), ((), ())), preferred_element_type=F32)
    colors = colors.astype(BF16).astype(F32)
    lane = lane_ids(8)
    p, q = (lane // 32) % 2, lane % 2
    for i in range(MAXT):
        source = (lane // 64) * span + i * TW + (lane % 32) // 2
        pixel = jnp.zeros((8, LANES), F32)
        for pq in range(4):
            found = jnp.take_along_axis(colors[8 * pq : 8 * pq + 8], source, axis=1)
            pixel = jnp.where(2 * p + q == pq, found, pixel)
        pixel = jnp.where(i < count[0, 0], pixel, 0.0).astype(BF16)
        for e in range(3):
            out[0, e, 0, i : i + 1] = pixel[e : e + 1]


def in_hbm(x):
    return pltpu.with_memory_space_constraint(x, pltpu.HBM)


def swapped(x):
    return lax.ppermute(x, "chan", [(0, 1), (1, 0)])


def spread(x, first, second):
    pairs = []
    for at in range(lax.axis_size("seq")):
        pairs.append((2 * at, 2 * (at ^ first)))
        pairs.append((2 * at + 1, 2 * (at ^ second) + 1))
    return lax.ppermute(x, ("seq", "chan"), pairs)


def local(latents, conv_in, conv_up, to_pixels, slot_anchor, slot_count):
    n = lax.axis_size("seq")
    current = latents[0]
    shard = current.shape[1]
    anchor = slot_anchor.transpose(1, 0, 2)
    in_flat = conv_in.reshape(-1, conv_in.shape[-1])
    pix = to_pixels.T
    routes = [(2 * k - 1, 2 * k) for k in range(1, n // 2)] + [(n - 1, n - 1)]
    anchors = [spread(anchor, *route) for route in routes]
    tm_size = lax.axis_size("tm")
    previous = lax.ppermute(current, "tm", [(i, i + 1) for i in range(tm_size - 1)])
    other_in, other_up = swapped(in_flat), swapped(conv_up)
    padded = (shard - 1) // LANES * LANES + 2 * LANES
    own = (current, anchor, in_flat, pix, conv_up)
    cur_pad, anchor, own_in, own_pix, own_up = pl.pallas_call(
        stage,
        out_shape=[
            jax.ShapeDtypeStruct((C_LAT, padded), BF16),
            *(jax.ShapeDtypeStruct(x.shape, x.dtype) for x in own[1:]),
        ],
        in_specs=[HBM] * 5,
        out_specs=[VMEM] * 5,
        scratch_shapes=[
            pltpu.VMEM(current.shape, BF16),
            pltpu.SemaphoreType.DMA((5,)),
        ],
        compiler_params=pltpu.CompilerParams(vmem_limit_bytes=8 << 20),
        cost_estimate=pl.CostEstimate(flops=1, bytes_accessed=1, transcendentals=0),
        name="stage",
    )(*map(in_hbm, own))
    plain = jax.ShapeDtypeStruct((ROOM, C_LAT, LANES), BF16)
    extended = jax.ShapeDtypeStruct((ROOM + 1, C_LAT, LANES), BF16)
    cut = []
    for targets, shape, name in (([anchor], plain, "cut_own"), (anchors, extended, "cut_windows")):
        cut += pl.pallas_call(
            functools.partial(cut_windows, n),
            out_shape=[shape] * len(targets),
            in_specs=[VMEM] * (len(targets) + 3),
            out_specs=[VMEM] * len(targets),
            scratch_shapes=[pltpu.VMEM((C_LAT, padded), BF16)],
            compiler_params=pltpu.CompilerParams(vmem_limit_bytes=4 << 20),
            cost_estimate=pl.CostEstimate(flops=1, bytes_accessed=1, transcendentals=0),
            name=name,
        )(*targets, cur_pad, previous, own_pix)
    parts = [cut[0]]
    for message, route in zip(cut[1:], routes[:-1]):
        arrived = spread(message, *route)
        parts += [arrived, swapped(arrived)]
    parts.append(spread(cut[-1], *routes[-1]))
    pixels = pl.pallas_call(
        functools.partial(decode, n),
        out_shape=jax.ShapeDtypeStruct((1, 3, 1, MAXT, LANES), BF16),
        in_specs=[SMEM] + [VMEM] * (n + 6),
        out_specs=VMEM,
        scratch_shapes=[
            pltpu.VMEM((n,) + plain.shape, BF16),
        ]
        + [pltpu.VMEM(((TH + 2) * MAXT, 4, WIDE, C_MID // 4), F32)] * TAPS
        + [pltpu.VMEM((TAPS, (TH + 2) * MAXT * TW, C_MID), BF16)] * TAPS,
        compiler_params=pltpu.CompilerParams(vmem_limit_bytes=32 << 20),
        name="decode",
    )(slot_count, anchor, *parts, own_in, other_in, own_pix, own_up, other_up)
    return pixels.transpose(0, 3, 1, 2, 4)


def solution(mesh):
    placed = (
        P(("clip", "tm"), None, "seq"),
        P(None, None, None, None, "chan"),
        P(None, None, None, None, "chan"),
        P("chan", None),
        P(("clip", "tm"), None, "seq"),
        P(("clip", "tm"), "seq"),
    )
    return jax.shard_map(
        local,
        mesh=mesh,
        in_specs=placed,
        out_specs=P(("clip", "tm"), "seq", None, None, None),
        check_vma=False,
    )
```

```python
import functools

import jax
import jax.numpy as jnp
from jax import lax
from jax.experimental import pallas as pl
from jax.experimental.pallas import tpu as pltpu
from jax.sharding import PartitionSpec as P

H_LAT = 45
W_LAT = 160
C_LAT = 16
C_MID = 512
FG = 4
TH = 2
TW = 16
MAXT = 4
ROWS = TH + 4
COLS = TW + 4
LANES = 128
TAPS = 3
WIDE = 24
ROOM = 2 * MAXT
BF16 = jnp.bfloat16
F32 = jnp.float32
VMEM = pl.BlockSpec(memory_space=pltpu.VMEM)
SMEM = pl.BlockSpec(memory_space=pltpu.SMEM)
HBM = pl.BlockSpec(memory_space=pltpu.HBM)
ANY = pl.BlockSpec(memory_space=pl.ANY)


def lane_ids(rows):
    return lax.broadcasted_iota(jnp.int32, (rows, LANES), 1)


def silu(v):
    return v * (0.5 * jnp.tanh(0.5 * v) + 0.5)


def fetched(sources, targets, sems):
    copies = [pltpu.make_async_copy(*pair, sems.at[i]) for i, pair in enumerate(zip(sources, targets))]
    for copy in copies:
        copy.start()
    return copies


def stage(*refs):
    sources, (cur_out, *outs, cur, sems) = refs[:5], refs[5:]
    copies = []
    for i, pair in enumerate(zip(sources, (cur, *outs))):
        copies.append(pltpu.make_async_copy(*pair, sems.at[i]))
        copies[i].start()
    copies[0].wait()
    cur_out[:, : cur.shape[1]] = cur[...]
    for copy in copies[1:]:
        copy.wait()


def cut_windows(n, *refs):
    count = (len(refs) - 4) // 2
    anchors, (cur, prev_ref, pix), outs, prev = refs[:count], refs[count : count + 3], refs[count + 3 : -1], refs[-1]
    shard = prev_ref.shape[1]
    per_frame = n // FG
    part_start = lax.rem(lax.axis_index("seq"), per_frame) * shard
    last_base = (shard - 1) // LANES * LANES
    lane = lane_ids(C_LAT)
    real = lax.axis_index("tm") > 0
    prev[:, :shard] = jnp.where(real, prev_ref[...], jnp.zeros((), BF16))
    for k in range(count):
        anchor = anchors[k][...]
        for i in range(MAXT):
            row0 = anchor[1, 0, i] - 2
            col0 = anchor[2, 0, i] - 2
            first = jnp.maximum(-col0, 0)
            end = jnp.minimum(W_LAT - col0, COLS)
            totals = [jnp.zeros((C_LAT, LANES), BF16)] * 2
            for rho in range(ROWS):
                start = (row0 + rho) * W_LAT + col0 - part_start
                base = jnp.clip(start & -LANES, 0, last_base)
                base = pl.multiple_of(base, LANES)
                off = start - base
                from_low = lane >= off
                least = COLS * rho + jnp.maximum(first, -start)
                past = COLS * rho + jnp.minimum(end, shard - start)
                keep = (lane >= least) & (lane < past)
                for half, source in enumerate((prev, cur)):
                    low = source[:, pl.ds(base, LANES)]
                    high = source[:, pl.ds(base + LANES, LANES)]
                    moved = pltpu.roll(jnp.where(from_low, low, high), (COLS * rho - off) & (LANES - 1), 1)
                    totals[half] = jnp.where(keep, moved, totals[half])
            for half in range(2):
                outs[k][half * MAXT + i] = totals[half]
    for out in outs if outs[0].shape[0] > ROOM else ():
        out[ROOM] = jnp.concatenate([pix[...], jnp.zeros((C_LAT - pix.shape[0], LANES), BF16)], axis=0)


def decode(n, *refs):
    count, anchor, parts = refs[0], refs[1][...], refs[2 : n + 2]
    own_in, other_in, own_pix, own_up, other_up, out, held, *scratch = refs[n + 2 :]
    hiddens, lineds = scratch[:TAPS], scratch[TAPS:]
    per_frame = n // FG
    me = lax.axis_index("seq")
    core = lax.axis_index("chan")
    held[me] = parts[0][...]
    for k in range(1, n // 2):
        held[me ^ (2 * k - 1 + core)] = parts[2 * k - 1][:ROOM]
        held[me ^ (2 * k - core)] = parts[2 * k][:ROOM]
    held[me ^ (n - 1)] = parts[n - 1][:ROOM]
    lane = lane_ids(C_LAT)

    def frame(j):
        pieces = []
        for i in range(MAXT):
            at = jnp.clip(anchor[0, 0, i], 0, FG - 1) + j
            late, rank = at // FG, lax.rem(at, FG) * per_frame
            piece = held[rank, late * MAXT + i]
            for p in range(1, per_frame):
                piece += held[rank + p, late * MAXT + i]
            pieces.append(piece)
        result = []
        for rho in range(ROWS):
            total = None
            for i, piece in enumerate(pieces):
                by = (WIDE * i - COLS * rho) % LANES
                piece = pltpu.roll(piece, by, 1) if by else piece
                total = piece if i == 0 else jnp.where(lane >= WIDE * i, piece, total)
            result.append([total] + [pltpu.roll(total, LANES - c, 1) for c in range(1, TAPS)])
        return result

    def turned(pieces):
        zeros = [jnp.zeros((C_LAT, LANES), BF16)] * (LANES // C_LAT - len(pieces))
        return jnp.concatenate(pieces + zeros, axis=0).T[: MAXT * WIDE]

    taps = [(b, c) for b in range(TAPS) for c in range(TAPS)]
    spots = range(TH + 2)
    frames = [frame(j) for j in range(TAPS + 2)]
    cells = [
        jnp.concatenate([turned([frames[j][r + b][c] for b, c in taps[:-1]]) for r in spots], axis=0)
        for j in range(TAPS + 2)
    ]
    tail = jnp.concatenate([turned([frames[j][r + 2][2] for j in range(TAPS + 2)]) for r in spots], axis=0)
    x = lax.broadcasted_iota(jnp.int32, (WIDE, LANES), 0)
    quarter, half = C_MID // 4, C_MID // 2
    for t in range(TAPS):
        volume = jnp.concatenate([*cells[t : t + TAPS], tail], axis=1)
        hidden, lined = hiddens[t], lineds[t]
        for first, weights in enumerate((own_in, other_in)):
            per_tap = len(taps) * C_LAT
            kernel = [weights[a * per_tap : a * per_tap + LANES] for a in range(TAPS)]
            for j in range(LANES // C_LAT):
                a = j - t
                ends = weights[a * per_tap + LANES : (a + 1) * per_tap] if 0 <= a < TAPS else None
                kernel.append(jnp.zeros((C_LAT, half), BF16) if ends is None else ends)
            pre = jnp.dot(volume, jnp.concatenate(kernel, axis=0), preferred_element_type=F32)
            for r in spots:
                for i in range(MAXT):
                    row = anchor[1, 0, i] - 1 + r
                    col = anchor[2, 0, i] - 1 + x
                    width = jnp.where((row >= 0) & (row < H_LAT), W_LAT, 0)
                    at = (r * MAXT + i) * WIDE
                    value = silu(pre[at : at + WIDE])
                    for q in range(2):
                        hidden[r * MAXT + i, 2 * first + q] = jnp.where(
                            (col >= 0) & (col < width), value[:, q * quarter : (q + 1) * quarter], 0.0
                        )
        for c in range(TAPS):
            for ri in range((TH + 2) * MAXT):
                for q in range(4):
                    lined[c, ri * TW : (ri + 1) * TW, q * quarter : (q + 1) * quarter] = hidden[
                        ri, q, c : c + TW
                    ].astype(BF16)
    outs = own_up.shape[-1]
    span = MAXT * TW
    total = jnp.zeros((TH * span, 2 * outs), F32)
    for a in range(TAPS):
        for c in range(TAPS):
            for b in range(TAPS):
                rows = lineds[a][c, b * span : (b + TH) * span]
                for first in range(2):
                    here = pl.ds(pl.multiple_of((first ^ core) * half, half), half)
                    weights = jnp.concatenate([own_up[a, b, c, here], other_up[a, b, c, here]], axis=1)
                    total += jnp.dot(rows[:, first * half : (first + 1) * half], weights, preferred_element_type=F32)
    upper = silu(total).astype(BF16)
    row = lax.broadcasted_iota(jnp.int32, (32, 12), 0)
    col = lax.broadcasted_iota(jnp.int32, (32, 12), 1)
    pick = ((row % 8) * 4 + row // 8 == col) & (row % 8 < 3)
    pix = jnp.concatenate([own_pix[...], parts[2][ROOM, : own_pix.shape[0]]], axis=1)
    pix = jnp.dot(pick.astype(BF16), pix, preferred_element_type=F32).astype(BF16)
    colors = lax.dot_general(pix, upper, (((1,), (1,)), ((), ())), preferred_element_type=F32)
    colors = colors.astype(BF16).astype(F32)
    lane = lane_ids(8)
    p, q = (lane // 32) % 2, lane % 2
    for i in range(MAXT):
        source = (lane // 64) * span + i * TW + (lane % 32) // 2
        pixel = jnp.zeros((8, LANES), F32)
        for pq in range(4):
            found = jnp.take_along_axis(colors[8 * pq : 8 * pq + 8], source, axis=1)
            pixel = jnp.where(2 * p + q == pq, found, pixel)
        pixel = jnp.where(i < count[0, 0], pixel, 0.0).astype(BF16)
        for e in range(3):
            out[0, e, 0, i : i + 1] = pixel[e : e + 1]


def in_hbm(x):
    return pltpu.with_memory_space_constraint(x, pltpu.HBM)


def swapped(x):
    return lax.ppermute(x, "chan", [(0, 1), (1, 0)])


def spread(x, first, second):
    pairs = []
    for at in range(lax.axis_size("seq")):
        pairs.append((2 * at, 2 * (at ^ first)))
        pairs.append((2 * at + 1, 2 * (at ^ second) + 1))
    return lax.ppermute(x, ("seq", "chan"), pairs)


def local(latents, conv_in, conv_up, to_pixels, slot_anchor, slot_count):
    n = lax.axis_size("seq")
    current = latents[0]
    shard = current.shape[1]
    anchor = slot_anchor.transpose(1, 0, 2)
    in_flat = conv_in.reshape(-1, conv_in.shape[-1])
    pix = to_pixels.T
    routes = [(2 * k - 1, 2 * k) for k in range(1, n // 2)] + [(n - 1, n - 1)]
    anchors = [spread(anchor, *route) for route in routes]
    tm_size = lax.axis_size("tm")
    previous = lax.ppermute(current, "tm", [(i, (i + 1) % tm_size) for i in range(tm_size)])
    other_in, other_up = swapped(in_flat), swapped(conv_up)
    padded = (shard - 1) // LANES * LANES + 2 * LANES
    own = (current, anchor, in_flat, pix, conv_up)
    cur_pad, anchor, own_in, own_pix, own_up = pl.pallas_call(
        stage,
        out_shape=[
            jax.ShapeDtypeStruct((C_LAT, padded), BF16),
            *(jax.ShapeDtypeStruct(x.shape, x.dtype) for x in own[1:]),
        ],
        in_specs=[HBM] * 5,
        out_specs=[VMEM] * 5,
        scratch_shapes=[
            pltpu.VMEM(current.shape, BF16),
            pltpu.SemaphoreType.DMA((5,)),
        ],
        compiler_params=pltpu.CompilerParams(vmem_limit_bytes=8 << 20),
        cost_estimate=pl.CostEstimate(flops=1, bytes_accessed=1, transcendentals=0),
        name="stage",
    )(*map(in_hbm, own))
    plain = jax.ShapeDtypeStruct((ROOM, C_LAT, LANES), BF16)
    extended = jax.ShapeDtypeStruct((ROOM + 1, C_LAT, LANES), BF16)
    cut = []
    for targets, shape, name in (([anchor], plain, "cut_own"), (anchors, extended, "cut_windows")):
        cut += pl.pallas_call(
            functools.partial(cut_windows, n),
            out_shape=[shape] * len(targets),
            in_specs=[VMEM] * (len(targets) + 3),
            out_specs=[VMEM] * len(targets),
            scratch_shapes=[pltpu.VMEM((C_LAT, padded), BF16)],
            compiler_params=pltpu.CompilerParams(vmem_limit_bytes=4 << 20),
            cost_estimate=pl.CostEstimate(flops=1, bytes_accessed=1, transcendentals=0),
            name=name,
        )(*targets, cur_pad, previous, own_pix)
    parts = [cut[0]]
    for message, route in zip(cut[1:], routes[:-1]):
        arrived = spread(message, *route)
        parts += [arrived, swapped(arrived)]
    parts.append(spread(cut[-1], *routes[-1]))
    pixels = pl.pallas_call(
        functools.partial(decode, n),
        out_shape=jax.ShapeDtypeStruct((1, 3, 1, MAXT, LANES), BF16),
        in_specs=[SMEM] + [VMEM] * (n + 6),
        out_specs=VMEM,
        scratch_shapes=[
            pltpu.VMEM((n,) + plain.shape, BF16),
        ]
        + [pltpu.VMEM(((TH + 2) * MAXT, 4, WIDE, C_MID // 4), F32)] * TAPS
        + [pltpu.VMEM((TAPS, (TH + 2) * MAXT * TW, C_MID), BF16)] * TAPS,
        compiler_params=pltpu.CompilerParams(vmem_limit_bytes=32 << 20),
        name="decode",
    )(slot_count, anchor, *parts, own_in, other_in, own_pix, own_up, other_up)
    return pixels.transpose(0, 3, 1, 2, 4)


def solution(mesh):
    placed = (
        P(("clip", "tm"), None, "seq"),
        P(None, None, None, None, "chan"),
        P(None, None, None, None, "chan"),
        P("chan", None),
        P(("clip", "tm"), None, "seq"),
        P(("clip", "tm"), "seq"),
    )
    return jax.shard_map(
        local,
        mesh=mesh,
        in_specs=placed,
        out_specs=P(("clip", "tm"), "seq", None, None, None),
        check_vma=False,
    )
```

```python
import functools

import jax
import jax.numpy as jnp
from jax import lax
from jax.experimental import pallas as pl
from jax.experimental.pallas import tpu as pltpu
from jax.sharding import PartitionSpec as P

H_LAT = 45
W_LAT = 160
C_LAT = 16
C_MID = 512
FG = 4
TH = 2
TW = 16
MAXT = 4
ROWS = TH + 4
COLS = TW + 4
LANES = 128
TAPS = 3
WIDE = 24
ROOM = 2 * MAXT
BF16 = jnp.bfloat16
F32 = jnp.float32
VMEM = pl.BlockSpec(memory_space=pltpu.VMEM)
SMEM = pl.BlockSpec(memory_space=pltpu.SMEM)
HBM = pl.BlockSpec(memory_space=pltpu.HBM)
ANY = pl.BlockSpec(memory_space=pl.ANY)


def lane_ids(rows):
    return lax.broadcasted_iota(jnp.int32, (rows, LANES), 1)


def silu(v):
    return v * (0.5 * jnp.tanh(0.5 * v) + 0.5)


def fetched(sources, targets, sems):
    copies = [pltpu.make_async_copy(*pair, sems.at[i]) for i, pair in enumerate(zip(sources, targets))]
    for copy in copies:
        copy.start()
    return copies


def stage(*refs):
    sources, (cur_out, *outs, cur, sems) = refs[:5], refs[5:]
    copies = []
    for i, pair in enumerate(zip(sources, (cur, *outs))):
        copies.append(pltpu.make_async_copy(*pair, sems.at[i]))
        copies[i].start()
    copies[0].wait()
    cur_out[:, : cur.shape[1]] = cur[...]
    for copy in copies[1:]:
        copy.wait()


def cut_windows(n, *refs):
    count = (len(refs) - 4) // 2
    anchors, (cur, prev_ref, pix), outs, prev = refs[:count], refs[count : count + 3], refs[count + 3 : -1], refs[-1]
    shard = prev_ref.shape[1]
    per_frame = n // FG
    part_start = lax.rem(lax.axis_index("seq"), per_frame) * shard
    last_base = (shard - 1) // LANES * LANES
    lane = lane_ids(C_LAT)
    real = lax.axis_index("tm") > 0
    prev[:, :shard] = jnp.where(real, prev_ref[...], jnp.zeros((), BF16))
    for k in range(count):
        anchor = anchors[k][...]
        for i in range(MAXT):
            row0 = anchor[1, 0, i] - 2
            col0 = anchor[2, 0, i] - 2
            first = jnp.maximum(-col0, 0)
            end = jnp.minimum(W_LAT - col0, COLS)
            totals = [jnp.zeros((C_LAT, LANES), BF16)] * 2
            for rho in range(ROWS):
                start = (row0 + rho) * W_LAT + col0 - part_start
                base = jnp.clip(start & -LANES, 0, last_base)
                base = pl.multiple_of(base, LANES)
                off = start - base
                from_low = lane >= off
                least = COLS * rho + jnp.maximum(first, -start)
                past = COLS * rho + jnp.minimum(end, shard - start)
                keep = (lane >= least) & (lane < past)
                for half, source in enumerate((prev, cur)):
                    low = source[:, pl.ds(base, LANES)]
                    high = source[:, pl.ds(base + LANES, LANES)]
                    moved = pltpu.roll(jnp.where(from_low, low, high), (COLS * rho - off) & (LANES - 1), 1)
                    totals[half] = jnp.where(keep, moved, totals[half])
            for half in range(2):
                outs[k][half * MAXT + i] = totals[half]
    for out in outs if outs[0].shape[0] > ROOM else ():
        out[ROOM] = jnp.concatenate([pix[...], jnp.zeros((C_LAT - pix.shape[0], LANES), BF16)], axis=0)


def decode(n, *refs):
    count, anchor, parts = refs[0], refs[1][...], refs[2 : n + 2]
    own_in, other_in, own_pix, own_up, other_up, out, held, *lineds = refs[n + 2 :]
    per_frame = n // FG
    me = lax.axis_index("seq")
    core = lax.axis_index("chan")
    held[me] = parts[0][...]
    for k in range(1, n // 2):
        held[me ^ (2 * k - 1 + core)] = parts[2 * k - 1][:ROOM]
        held[me ^ (2 * k - core)] = parts[2 * k][:ROOM]
    held[me ^ (n - 1)] = parts[n - 1][:ROOM]
    lane = lane_ids(C_LAT)

    firsts = [anchor[0, 0, i] & (FG - 1) for i in range(MAXT)]

    def frame(j):
        pieces = []
        for i in range(MAXT):
            at = firsts[i] + j
            late, rank = at >> 2, (at & (FG - 1)) * per_frame
            piece = held[rank, late * MAXT + i]
            for p in range(1, per_frame):
                piece += held[rank + p, late * MAXT + i]
            pieces.append(piece)
        result = []
        for rho in range(ROWS):
            total = None
            for i, piece in enumerate(pieces):
                by = (WIDE * i - COLS * rho) % LANES
                piece = pltpu.roll(piece, by, 1) if by else piece
                total = piece if i == 0 else jnp.where(lane >= WIDE * i, piece, total)
            result.append([total] + [pltpu.roll(total, LANES - c, 1) for c in range(1, TAPS)])
        return result

    def turned(pieces):
        zeros = [jnp.zeros((C_LAT, LANES), BF16)] * (LANES // C_LAT - len(pieces))
        return jnp.concatenate(pieces + zeros, axis=0).T[: MAXT * WIDE]

    taps = [(b, c) for b in range(TAPS) for c in range(TAPS)]
    spots = range(TH + 2)
    frames = [frame(j) for j in range(TAPS + 2)]
    cells = [
        jnp.concatenate([turned([frames[j][r + b][c] for b, c in taps[:-1]]) for r in spots], axis=0)
        for j in range(TAPS + 2)
    ]
    tail = jnp.concatenate([turned([frames[j][r + 2][2] for j in range(TAPS + 2)]) for r in spots], axis=0)
    x = lax.broadcasted_iota(jnp.int32, (WIDE, LANES), 0)
    quarter, half = C_MID // 4, C_MID // 2
    for t in range(TAPS):
        volume = jnp.concatenate([*cells[t : t + TAPS], tail], axis=1)
        lined = lineds[t]
        for first, weights in enumerate((own_in, other_in)):
            per_tap = len(taps) * C_LAT
            kernel = [weights[a * per_tap : a * per_tap + LANES] for a in range(TAPS)]
            for j in range(LANES // C_LAT):
                a = j - t
                ends = weights[a * per_tap + LANES : (a + 1) * per_tap] if 0 <= a < TAPS else None
                kernel.append(jnp.zeros((C_LAT, half), BF16) if ends is None else ends)
            pre = jnp.dot(volume, jnp.concatenate(kernel, axis=0), preferred_element_type=F32)
            for r in spots:
                for i in range(MAXT):
                    row = anchor[1, 0, i] - 1 + r
                    col = anchor[2, 0, i] - 1 + x
                    width = jnp.where((row >= 0) & (row < H_LAT), W_LAT, 0)
                    at = (r * MAXT + i) * WIDE
                    value = silu(pre[at : at + WIDE])
                    for q in range(2):
                        part = slice((2 * first + q) * quarter, (2 * first + q + 1) * quarter)
                        kept = jnp.where((col >= 0) & (col < width), value[:, q * quarter : (q + 1) * quarter], 0.0)
                        for c in range(TAPS):
                            moved = pltpu.roll(kept, WIDE - c, 0) if c else kept
                            lined[c, (r * MAXT + i) * TW : (r * MAXT + i + 1) * TW, part] = moved[:TW].astype(BF16)
    outs = own_up.shape[-1]
    span = MAXT * TW
    total = jnp.zeros((TH * span, 2 * outs), F32)
    for a in range(TAPS):
        for c in range(TAPS):
            for b in range(TAPS):
                rows = lineds[a][c, b * span : (b + TH) * span]
                for first in range(2):
                    here = pl.ds(pl.multiple_of((first ^ core) * half, half), half)
                    weights = jnp.concatenate([own_up[a, b, c, here], other_up[a, b, c, here]], axis=1)
                    total += jnp.dot(rows[:, first * half : (first + 1) * half], weights, preferred_element_type=F32)
    upper = silu(total).astype(BF16)
    row = lax.broadcasted_iota(jnp.int32, (32, 12), 0)
    col = lax.broadcasted_iota(jnp.int32, (32, 12), 1)
    pick = ((row % 8) * 4 + row // 8 == col) & (row % 8 < 3)
    pix = jnp.concatenate([own_pix[...], parts[2][ROOM, : own_pix.shape[0]]], axis=1)
    pix = jnp.dot(pick.astype(BF16), pix, preferred_element_type=F32).astype(BF16)
    colors = lax.dot_general(pix, upper, (((1,), (1,)), ((), ())), preferred_element_type=F32)
    colors = colors.astype(BF16).astype(F32)
    lane = lane_ids(8)
    p, q = (lane // 32) % 2, lane % 2
    for i in range(MAXT):
        source = (lane // 64) * span + i * TW + (lane % 32) // 2
        pixel = jnp.zeros((8, LANES), F32)
        for pq in range(4):
            found = jnp.take_along_axis(colors[8 * pq : 8 * pq + 8], source, axis=1)
            pixel = jnp.where(2 * p + q == pq, found, pixel)
        pixel = jnp.where(i < count[0, 0], pixel, 0.0).astype(BF16)
        for e in range(3):
            out[0, e, 0, i : i + 1] = pixel[e : e + 1]


def in_hbm(x):
    return pltpu.with_memory_space_constraint(x, pltpu.HBM)


def swapped(x):
    return lax.ppermute(x, "chan", [(0, 1), (1, 0)])


def spread(x, first, second):
    pairs = []
    for at in range(lax.axis_size("seq")):
        pairs.append((2 * at, 2 * (at ^ first)))
        pairs.append((2 * at + 1, 2 * (at ^ second) + 1))
    return lax.ppermute(x, ("seq", "chan"), pairs)


def local(latents, conv_in, conv_up, to_pixels, slot_anchor, slot_count):
    n = lax.axis_size("seq")
    current = latents[0]
    shard = current.shape[1]
    anchor = slot_anchor.transpose(1, 0, 2)
    in_flat = conv_in.reshape(-1, conv_in.shape[-1])
    pix = to_pixels.T
    routes = [(2 * k - 1, 2 * k) for k in range(1, n // 2)] + [(n - 1, n - 1)]
    anchors = [spread(anchor, *route) for route in routes]
    tm_size = lax.axis_size("tm")
    previous = lax.ppermute(current, "tm", [(i, (i + 1) % tm_size) for i in range(tm_size)])
    other_in, other_up = swapped(in_flat), swapped(conv_up)
    padded = (shard - 1) // LANES * LANES + 2 * LANES
    own = (current, anchor, in_flat, pix, conv_up)
    cur_pad, anchor, own_in, own_pix, own_up = pl.pallas_call(
        stage,
        out_shape=[
            jax.ShapeDtypeStruct((C_LAT, padded), BF16),
            *(jax.ShapeDtypeStruct(x.shape, x.dtype) for x in own[1:]),
        ],
        in_specs=[HBM] * 5,
        out_specs=[VMEM] * 5,
        scratch_shapes=[
            pltpu.VMEM(current.shape, BF16),
            pltpu.SemaphoreType.DMA((5,)),
        ],
        compiler_params=pltpu.CompilerParams(vmem_limit_bytes=8 << 20),
        cost_estimate=pl.CostEstimate(flops=1, bytes_accessed=1, transcendentals=0),
        name="stage",
    )(*map(in_hbm, own))
    plain = jax.ShapeDtypeStruct((ROOM, C_LAT, LANES), BF16)
    extended = jax.ShapeDtypeStruct((ROOM + 1, C_LAT, LANES), BF16)
    cut = []
    for targets, shape, name in (([anchor], plain, "cut_own"), (anchors, extended, "cut_windows")):
        cut += pl.pallas_call(
            functools.partial(cut_windows, n),
            out_shape=[shape] * len(targets),
            in_specs=[VMEM] * (len(targets) + 3),
            out_specs=[VMEM] * len(targets),
            scratch_shapes=[pltpu.VMEM((C_LAT, padded), BF16)],
            compiler_params=pltpu.CompilerParams(vmem_limit_bytes=4 << 20),
            cost_estimate=pl.CostEstimate(flops=1, bytes_accessed=1, transcendentals=0),
            name=name,
        )(*targets, cur_pad, previous, own_pix)
    parts = [cut[0]]
    for message, route in zip(cut[1:], routes[:-1]):
        arrived = spread(message, *route)
        parts += [arrived, swapped(arrived)]
    parts.append(spread(cut[-1], *routes[-1]))
    pixels = pl.pallas_call(
        functools.partial(decode, n),
        out_shape=jax.ShapeDtypeStruct((1, 3, 1, MAXT, LANES), BF16),
        in_specs=[SMEM] + [VMEM] * (n + 6),
        out_specs=VMEM,
        scratch_shapes=[
            pltpu.VMEM((n,) + plain.shape, BF16),
        ]
        + [pltpu.VMEM((TAPS, (TH + 2) * MAXT * TW, C_MID), BF16)] * TAPS,
        compiler_params=pltpu.CompilerParams(vmem_limit_bytes=32 << 20),
        name="decode",
    )(slot_count, anchor, *parts, own_in, other_in, own_pix, own_up, other_up)
    return pixels.transpose(0, 3, 1, 2, 4)


def solution(mesh):
    placed = (
        P(("clip", "tm"), None, "seq"),
        P(None, None, None, None, "chan"),
        P(None, None, None, None, "chan"),
        P("chan", None),
        P(("clip", "tm"), None, "seq"),
        P(("clip", "tm"), "seq"),
    )
    return jax.shard_map(
        local,
        mesh=mesh,
        in_specs=placed,
        out_specs=P(("clip", "tm"), "seq", None, None, None),
        check_vma=False,
    )
```

```python
import functools

import jax
import jax.numpy as jnp
from jax import lax
from jax.experimental import pallas as pl
from jax.experimental.pallas import tpu as pltpu
from jax.sharding import PartitionSpec as P

H_LAT = 45
W_LAT = 160
C_LAT = 16
C_MID = 512
FG = 4
TH = 2
TW = 16
MAXT = 4
ROWS = TH + 4
COLS = TW + 4
LANES = 128
TAPS = 3
WIDE = 24
ROOM = 2 * MAXT
BF16 = jnp.bfloat16
F32 = jnp.float32
VMEM = pl.BlockSpec(memory_space=pltpu.VMEM)
SMEM = pl.BlockSpec(memory_space=pltpu.SMEM)
HBM = pl.BlockSpec(memory_space=pltpu.HBM)
ANY = pl.BlockSpec(memory_space=pl.ANY)


def lane_ids(rows):
    return lax.broadcasted_iota(jnp.int32, (rows, LANES), 1)


def silu(v):
    return v * (0.5 * jnp.tanh(0.5 * v) + 0.5)


def fetched(sources, targets, sems):
    copies = [pltpu.make_async_copy(*pair, sems.at[i]) for i, pair in enumerate(zip(sources, targets))]
    for copy in copies:
        copy.start()
    return copies


def stage(*refs):
    sources, (cur_out, *outs, cur, sems) = refs[:5], refs[5:]
    copies = []
    for i, pair in enumerate(zip(sources, (cur, *outs))):
        copies.append(pltpu.make_async_copy(*pair, sems.at[i]))
        copies[i].start()
    copies[0].wait()
    cur_out[:, : cur.shape[1]] = cur[...]
    for copy in copies[1:]:
        copy.wait()


def cut_windows(n, *refs):
    count = (len(refs) - 4) // 2
    anchors, (cur, prev_ref, pix), outs, prev = refs[:count], refs[count : count + 3], refs[count + 3 : -1], refs[-1]
    shard = prev_ref.shape[1]
    per_frame = n // FG
    part_start = lax.rem(lax.axis_index("seq"), per_frame) * shard
    last_base = (shard - 1) // LANES * LANES
    last_base = (shard - 1) // LANES * LANES
    lane = lane_ids(C_LAT)
    spot_row, spot_col = lane // COLS, lane % COLS
    spot = jnp.where(spot_row < ROWS, spot_row * W_LAT + spot_col, -H_LAT * W_LAT)
    of_row = [spot_row == rho for rho in range(ROWS)]
    real = lax.axis_index("tm") > 0
    prev[:, :shard] = jnp.where(real, prev_ref[...], jnp.zeros((), BF16))
    for k in range(count):
        anchor = anchors[k][...]
        for i in range(MAXT):
            col0 = anchor[2, 0, i] - 2
            origin = (anchor[1, 0, i] - 2) * W_LAT + col0 - part_start
            token, col = spot + origin, spot_col + col0
            keep = (token >= 0) & (token < shard) & (col >= 0) & (col < W_LAT)
            totals = [None, None]
            for rho in range(ROWS):
                start = origin + rho * W_LAT
                base = jnp.minimum(jnp.maximum(start & -LANES, 0), last_base)
                base = pl.multiple_of(base, LANES)
                off = start - base
                from_low = lane >= off
                for half, source in enumerate((prev, cur)):
                    low = source[:, pl.ds(base, LANES)]
                    high = source[:, pl.ds(base + LANES, LANES)]
                    moved = pltpu.roll(jnp.where(from_low, low, high), (COLS * rho - off) & (LANES - 1), 1)
                    totals[half] = moved if rho == 0 else jnp.where(of_row[rho], moved, totals[half])
            for half in range(2):
                outs[k][half * MAXT + i] = jnp.where(keep, totals[half], jnp.zeros((), BF16))
    for out in outs if outs[0].shape[0] > ROOM else ():
        out[ROOM] = jnp.concatenate([pix[...], jnp.zeros((C_LAT - pix.shape[0], LANES), BF16)], axis=0)


def decode(n, *refs):
    count, anchor, parts = refs[0], refs[1][...], refs[2 : n + 2]
    own_in, other_in, own_pix, own_up, other_up, out, held, *lineds = refs[n + 2 :]
    per_frame = n // FG
    me = lax.axis_index("seq")
    core = lax.axis_index("chan")
    held[me] = parts[0][...]
    routes = seq_routes(n)
    for k, (first, second) in enumerate(routes[:-1]):
        held[me ^ (first + core * (second - first))] = parts[2 * k + 1][:ROOM]
        held[me ^ (second + core * (first - second))] = parts[2 * k + 2][:ROOM]
    held[me ^ routes[-1][0]] = parts[n - 1][:ROOM]
    lane = lane_ids(C_LAT)

    firsts = [anchor[0, 0, i] & (FG - 1) for i in range(MAXT)]

    def frame(j):
        pieces = []
        for i in range(MAXT):
            at = firsts[i] + j
            late, rank = at >> 2, (at & (FG - 1)) * per_frame
            piece = held[rank, late * MAXT + i]
            for p in range(1, per_frame):
                piece += held[rank + p, late * MAXT + i]
            pieces.append(piece)
        result = []
        for rho in range(ROWS):
            total = None
            for i, piece in enumerate(pieces):
                by = (WIDE * i - COLS * rho) % LANES
                piece = pltpu.roll(piece, by, 1) if by else piece
                total = piece if i == 0 else jnp.where(lane >= WIDE * i, piece, total)
            result.append([total] + [pltpu.roll(total, LANES - c, 1) for c in range(1, TAPS)])
        return result

    def turned(pieces):
        zeros = [jnp.zeros((C_LAT, LANES), BF16)] * (LANES // C_LAT - len(pieces))
        return jnp.concatenate(pieces + zeros, axis=0).T[: MAXT * WIDE]

    taps = [(b, c) for b in range(TAPS) for c in range(TAPS)]
    spots = range(TH + 2)
    frames = [frame(j) for j in range(TAPS + 2)]
    cells = [
        jnp.concatenate([turned([frames[j][r + b][c] for b, c in taps[:-1]]) for r in spots], axis=0)
        for j in range(TAPS + 2)
    ]
    tail = jnp.concatenate([turned([frames[j][r + 2][2] for j in range(TAPS + 2)]) for r in spots], axis=0)
    x = lax.broadcasted_iota(jnp.int32, (WIDE, LANES), 0)
    quarter, half = C_MID // 4, C_MID // 2
    for t in range(TAPS):
        volume = jnp.concatenate([*cells[t : t + TAPS], tail], axis=1)
        lined = lineds[t]
        for first, weights in enumerate((own_in, other_in)):
            per_tap = len(taps) * C_LAT
            kernel = [weights[a * per_tap : a * per_tap + LANES] for a in range(TAPS)]
            for j in range(LANES // C_LAT):
                a = j - t
                ends = weights[a * per_tap + LANES : (a + 1) * per_tap] if 0 <= a < TAPS else None
                kernel.append(jnp.zeros((C_LAT, half), BF16) if ends is None else ends)
            pre = jnp.dot(volume, jnp.concatenate(kernel, axis=0), preferred_element_type=F32)
            for r in spots:
                for i in range(MAXT):
                    row = anchor[1, 0, i] - 1 + r
                    col = anchor[2, 0, i] - 1 + x
                    width = jnp.where((row >= 0) & (row < H_LAT), W_LAT, 0)
                    at = (r * MAXT + i) * WIDE
                    value = silu(pre[at : at + WIDE])
                    for q in range(2):
                        part = slice((2 * first + q) * quarter, (2 * first + q + 1) * quarter)
                        kept = jnp.where((col >= 0) & (col < width), value[:, q * quarter : (q + 1) * quarter], 0.0)
                        for c in range(TAPS):
                            moved = pltpu.roll(kept, WIDE - c, 0) if c else kept
                            lined[c, (r * MAXT + i) * TW : (r * MAXT + i + 1) * TW, part] = moved[:TW].astype(BF16)
    outs = own_up.shape[-1]
    span = MAXT * TW
    total = jnp.zeros((TH * span, 2 * outs), F32)
    for a in range(TAPS):
        for c in range(TAPS):
            for b in range(TAPS):
                rows = lineds[a][c, b * span : (b + TH) * span]
                for first in range(2):
                    here = pl.ds(pl.multiple_of((first ^ core) * half, half), half)
                    weights = jnp.concatenate([own_up[a, b, c, here], other_up[a, b, c, here]], axis=1)
                    total += jnp.dot(rows[:, first * half : (first + 1) * half], weights, preferred_element_type=F32)
    upper = silu(total).astype(BF16)
    row = lax.broadcasted_iota(jnp.int32, (32, 12), 0)
    col = lax.broadcasted_iota(jnp.int32, (32, 12), 1)
    pick = ((row % 8) * 4 + row // 8 == col) & (row % 8 < 3)
    pix = jnp.concatenate([own_pix[...], parts[2][ROOM, : own_pix.shape[0]]], axis=1)
    pix = jnp.dot(pick.astype(BF16), pix, preferred_element_type=F32).astype(BF16)
    colors = lax.dot_general(pix, upper, (((1,), (1,)), ((), ())), preferred_element_type=F32)
    colors = colors.astype(BF16).astype(F32)
    lane = lane_ids(8)
    p, q = (lane // 32) % 2, lane % 2
    for i in range(MAXT):
        source = (lane // 64) * span + i * TW + (lane % 32) // 2
        pixel = jnp.zeros((8, LANES), F32)
        for pq in range(4):
            found = jnp.take_along_axis(colors[8 * pq : 8 * pq + 8], source, axis=1)
            pixel = jnp.where(2 * p + q == pq, found, pixel)
        pixel = jnp.where(i < count[0, 0], pixel, 0.0).astype(BF16)
        for e in range(3):
            out[0, e, 0, i : i + 1] = pixel[e : e + 1]


def in_hbm(x):
    return pltpu.with_memory_space_constraint(x, pltpu.HBM)


def seq_routes(n):
    codes = [1, *range(3, n), 2]
    return list(zip(codes[:-1:2], codes[1:-1:2])) + [(codes[-1], codes[-1])]


def swapped(x):
    return lax.ppermute(x, "chan", [(0, 1), (1, 0)])


def spread(x, first, second):
    pairs = []
    for at in range(lax.axis_size("seq")):
        pairs.append((2 * at, 2 * (at ^ first)))
        pairs.append((2 * at + 1, 2 * (at ^ second) + 1))
    return lax.ppermute(x, ("seq", "chan"), pairs)


def local(latents, conv_in, conv_up, to_pixels, slot_anchor, slot_count):
    n = lax.axis_size("seq")
    current = latents[0]
    shard = current.shape[1]
    anchor = slot_anchor.transpose(1, 0, 2)
    in_flat = conv_in.reshape(-1, conv_in.shape[-1])
    pix = to_pixels.T
    routes = seq_routes(n)
    anchors = [spread(anchor, *route) for route in routes]
    tm_size = lax.axis_size("tm")
    previous = lax.ppermute(current, "tm", [(i, (i + 1) % tm_size) for i in range(tm_size)])
    other_in, other_up = swapped(in_flat), swapped(conv_up)
    padded = (shard - 1) // LANES * LANES + 2 * LANES
    own = (current, anchor, in_flat, pix, conv_up)
    cur_pad, anchor, own_in, own_pix, own_up = pl.pallas_call(
        stage,
        out_shape=[
            jax.ShapeDtypeStruct((C_LAT, padded), BF16),
            *(jax.ShapeDtypeStruct(x.shape, x.dtype) for x in own[1:]),
        ],
        in_specs=[HBM] * 5,
        out_specs=[VMEM] * 5,
        scratch_shapes=[
            pltpu.VMEM(current.shape, BF16),
            pltpu.SemaphoreType.DMA((5,)),
        ],
        compiler_params=pltpu.CompilerParams(vmem_limit_bytes=8 << 20),
        cost_estimate=pl.CostEstimate(flops=1, bytes_accessed=1, transcendentals=0),
        name="stage",
    )(*map(in_hbm, own))
    plain = jax.ShapeDtypeStruct((ROOM, C_LAT, LANES), BF16)
    extended = jax.ShapeDtypeStruct((ROOM + 1, C_LAT, LANES), BF16)
    cut = []
    for targets, shape, name in (([anchor], plain, "cut_own"), (anchors, extended, "cut_windows")):
        cut += pl.pallas_call(
            functools.partial(cut_windows, n),
            out_shape=[shape] * len(targets),
            in_specs=[VMEM] * (len(targets) + 3),
            out_specs=[VMEM] * len(targets),
            scratch_shapes=[pltpu.VMEM((C_LAT, padded), BF16)],
            compiler_params=pltpu.CompilerParams(vmem_limit_bytes=4 << 20),
            cost_estimate=pl.CostEstimate(flops=1, bytes_accessed=1, transcendentals=0),
            name=name,
        )(*targets, cur_pad, previous, own_pix)
    parts = [cut[0]]
    for message, route in zip(cut[1:], routes[:-1]):
        arrived = spread(message, *route)
        parts += [arrived, swapped(arrived)]
    parts.append(spread(cut[-1], *routes[-1]))
    pixels = pl.pallas_call(
        functools.partial(decode, n),
        out_shape=jax.ShapeDtypeStruct((1, 3, 1, MAXT, LANES), BF16),
        in_specs=[SMEM] + [VMEM] * (n + 6),
        out_specs=VMEM,
        scratch_shapes=[
            pltpu.VMEM((n,) + plain.shape, BF16),
        ]
        + [pltpu.VMEM((TAPS, (TH + 2) * MAXT * TW, C_MID), BF16)] * TAPS,
        compiler_params=pltpu.CompilerParams(vmem_limit_bytes=32 << 20),
        name="decode",
    )(slot_count, anchor, *parts, own_in, other_in, own_pix, own_up, other_up)
    return pixels.transpose(0, 3, 1, 2, 4)


def solution(mesh):
    placed = (
        P(("clip", "tm"), None, "seq"),
        P(None, None, None, None, "chan"),
        P(None, None, None, None, "chan"),
        P("chan", None),
        P(("clip", "tm"), None, "seq"),
        P(("clip", "tm"), "seq"),
    )
    return jax.shard_map(
        local,
        mesh=mesh,
        in_specs=placed,
        out_specs=P(("clip", "tm"), "seq", None, None, None),
        check_vma=False,
    )
```

```python
import functools

import jax
import jax.numpy as jnp
from jax import lax
from jax.experimental import pallas as pl
from jax.experimental.pallas import tpu as pltpu
from jax.sharding import PartitionSpec as P

H_LAT = 45
W_LAT = 160
C_LAT = 16
C_MID = 512
FG = 4
TH = 2
TW = 16
MAXT = 4
ROWS = TH + 4
COLS = TW + 4
LANES = 128
TAPS = 3
WIDE = 24
ROOM = 2 * MAXT
BF16 = jnp.bfloat16
F32 = jnp.float32
VMEM = pl.BlockSpec(memory_space=pltpu.VMEM)
SMEM = pl.BlockSpec(memory_space=pltpu.SMEM)
HBM = pl.BlockSpec(memory_space=pltpu.HBM)
ANY = pl.BlockSpec(memory_space=pl.ANY)


def lane_ids(rows):
    return lax.broadcasted_iota(jnp.int32, (rows, LANES), 1)


def silu(v):
    return v * (0.5 * jnp.tanh(0.5 * v) + 0.5)


def fetched(sources, targets, sems):
    copies = [pltpu.make_async_copy(*pair, sems.at[i]) for i, pair in enumerate(zip(sources, targets))]
    for copy in copies:
        copy.start()
    return copies


def stage(*refs):
    sources, (cur_out, *outs, cur, sems) = refs[:5], refs[5:]
    copies = []
    for i, pair in enumerate(zip(sources, (cur, *outs))):
        copies.append(pltpu.make_async_copy(*pair, sems.at[i]))
        copies[i].start()
    copies[0].wait()
    cur_out[:, : cur.shape[1]] = cur[...]
    for copy in copies[1:]:
        copy.wait()


def cut_windows(n, *refs):
    count = (len(refs) - 3) // 2
    anchors, (cur, prev_ref), outs, prev = refs[:count], refs[count : count + 2], refs[count + 2 : -1], refs[-1]
    shard = prev_ref.shape[1]
    per_frame = n // FG
    part_start = lax.rem(lax.axis_index("seq"), per_frame) * shard
    last_base = (shard - 1) // LANES * LANES
    last_base = (shard - 1) // LANES * LANES
    lane = lane_ids(C_LAT)
    spot_row, spot_col = lane // COLS, lane % COLS
    spot = jnp.where(spot_row < ROWS, spot_row * W_LAT + spot_col, -H_LAT * W_LAT)
    of_row = [spot_row == rho for rho in range(ROWS)]
    real = lax.axis_index("tm") > 0
    prev[:, :shard] = jnp.where(real, prev_ref[...], jnp.zeros((), BF16))
    for k in range(count):
        anchor = anchors[k][...]
        for i in range(MAXT):
            col0 = anchor[2, 0, i] - 2
            origin = (anchor[1, 0, i] - 2) * W_LAT + col0 - part_start
            token, col = spot + origin, spot_col + col0
            keep = (token >= 0) & (token < shard) & (col >= 0) & (col < W_LAT)
            totals = [None, None]
            for rho in range(ROWS):
                start = origin + rho * W_LAT
                base = jnp.minimum(jnp.maximum(start & -LANES, 0), last_base)
                base = pl.multiple_of(base, LANES)
                off = start - base
                from_low = lane >= off
                for half, source in enumerate((prev, cur)):
                    low = source[:, pl.ds(base, LANES)]
                    high = source[:, pl.ds(base + LANES, LANES)]
                    moved = pltpu.roll(jnp.where(from_low, low, high), (COLS * rho - off) & (LANES - 1), 1)
                    totals[half] = moved if rho == 0 else jnp.where(of_row[rho], moved, totals[half])
            for half in range(2):
                outs[k][half * MAXT + i] = jnp.where(keep, totals[half], jnp.zeros((), BF16))


def decode(n, *refs):
    count, anchor, parts = refs[0], refs[1][...], refs[2 : n + 2]
    own_in, other_in, own_pix, other_pix, own_up, other_up, out, held, *lineds = refs[n + 2 :]
    per_frame = n // FG
    me = lax.axis_index("seq")
    core = lax.axis_index("chan")
    held[me] = parts[0][...]
    routes = seq_routes(n)
    for k, (first, second) in enumerate(routes[:-1]):
        held[me ^ (first + core * (second - first))] = parts[2 * k + 1][...]
        held[me ^ (second + core * (first - second))] = parts[2 * k + 2][...]
    held[me ^ routes[-1][0]] = parts[n - 1][...]
    lane = lane_ids(C_LAT)

    firsts = [anchor[0, 0, i] & (FG - 1) for i in range(MAXT)]

    def frame(j):
        pieces = []
        for i in range(MAXT):
            at = firsts[i] + j
            late, rank = at >> 2, (at & (FG - 1)) * per_frame
            piece = held[rank, late * MAXT + i]
            for p in range(1, per_frame):
                piece += held[rank + p, late * MAXT + i]
            pieces.append(piece)
        result = []
        for rho in range(ROWS):
            total = None
            for i, piece in enumerate(pieces):
                by = (WIDE * i - COLS * rho) % LANES
                piece = pltpu.roll(piece, by, 1) if by else piece
                total = piece if i == 0 else jnp.where(lane >= WIDE * i, piece, total)
            result.append([total] + [pltpu.roll(total, LANES - c, 1) for c in range(1, TAPS)])
        return result

    def turned(pieces):
        zeros = [jnp.zeros((C_LAT, LANES), BF16)] * (LANES // C_LAT - len(pieces))
        return jnp.concatenate(pieces + zeros, axis=0).T[: MAXT * WIDE]

    taps = [(b, c) for b in range(TAPS) for c in range(TAPS)]
    spots = range(TH + 2)
    frames = [frame(j) for j in range(TAPS + 2)]
    cells = [
        jnp.concatenate([turned([frames[j][r + b][c] for b, c in taps[:-1]]) for r in spots], axis=0)
        for j in range(TAPS + 2)
    ]
    tail = jnp.concatenate([turned([frames[j][r + 2][2] for j in range(TAPS + 2)]) for r in spots], axis=0)
    x = lax.broadcasted_iota(jnp.int32, (WIDE, LANES), 0)
    quarter, half = C_MID // 4, C_MID // 2
    for t in range(TAPS):
        volume = jnp.concatenate([*cells[t : t + TAPS], tail], axis=1)
        lined = lineds[t]
        for first, weights in enumerate((own_in, other_in)):
            per_tap = len(taps) * C_LAT
            kernel = [weights[a * per_tap : a * per_tap + LANES] for a in range(TAPS)]
            for j in range(LANES // C_LAT):
                a = j - t
                ends = weights[a * per_tap + LANES : (a + 1) * per_tap] if 0 <= a < TAPS else None
                kernel.append(jnp.zeros((C_LAT, half), BF16) if ends is None else ends)
            pre = jnp.dot(volume, jnp.concatenate(kernel, axis=0), preferred_element_type=F32)
            for r in spots:
                for i in range(MAXT):
                    row = anchor[1, 0, i] - 1 + r
                    col = anchor[2, 0, i] - 1 + x
                    width = jnp.where((row >= 0) & (row < H_LAT), W_LAT, 0)
                    at = (r * MAXT + i) * WIDE
                    value = silu(pre[at : at + WIDE])
                    for q in range(2):
                        part = slice((2 * first + q) * quarter, (2 * first + q + 1) * quarter)
                        kept = jnp.where((col >= 0) & (col < width), value[:, q * quarter : (q + 1) * quarter], 0.0)
                        for c in range(TAPS):
                            moved = pltpu.roll(kept, WIDE - c, 0) if c else kept
                            lined[c, (r * MAXT + i) * TW : (r * MAXT + i + 1) * TW, part] = moved[:TW].astype(BF16)
    outs = own_up.shape[-1]
    span = MAXT * TW
    total = jnp.zeros((TH * span, 2 * outs), F32)
    for a in range(TAPS):
        for c in range(TAPS):
            for b in range(TAPS):
                rows = lineds[a][c, b * span : (b + TH) * span]
                for first in range(2):
                    here = pl.ds(pl.multiple_of((first ^ core) * half, half), half)
                    weights = jnp.concatenate([own_up[a, b, c, here], other_up[a, b, c, here]], axis=1)
                    total += jnp.dot(rows[:, first * half : (first + 1) * half], weights, preferred_element_type=F32)
    upper = silu(total).astype(BF16)
    row = lax.broadcasted_iota(jnp.int32, (32, 12), 0)
    col = lax.broadcasted_iota(jnp.int32, (32, 12), 1)
    pick = ((row % 8) * 4 + row // 8 == col) & (row % 8 < 3)
    pix = jnp.concatenate([own_pix[...], other_pix[...]], axis=1)
    pix = jnp.dot(pick.astype(BF16), pix, preferred_element_type=F32).astype(BF16)
    colors = lax.dot_general(pix, upper, (((1,), (1,)), ((), ())), preferred_element_type=F32)
    colors = colors.astype(BF16).astype(F32)
    lane = lane_ids(8)
    p, q = (lane // 32) % 2, lane % 2
    for i in range(MAXT):
        source = (lane // 64) * span + i * TW + (lane % 32) // 2
        pixel = jnp.zeros((8, LANES), F32)
        for pq in range(4):
            found = jnp.take_along_axis(colors[8 * pq : 8 * pq + 8], source, axis=1)
            pixel = jnp.where(2 * p + q == pq, found, pixel)
        pixel = jnp.where(i < count[0, 0], pixel, 0.0).astype(BF16)
        for e in range(3):
            out[0, e, 0, i : i + 1] = pixel[e : e + 1]


def in_hbm(x):
    return pltpu.with_memory_space_constraint(x, pltpu.HBM)


def seq_routes(n):
    codes = [1, *range(3, n), 2]
    return list(zip(codes[:-1:2], codes[1:-1:2])) + [(codes[-1], codes[-1])]


def swapped(x):
    return lax.ppermute(x, "chan", [(0, 1), (1, 0)])


def spread(x, first, second):
    pairs = []
    for at in range(lax.axis_size("seq")):
        pairs.append((2 * at, 2 * (at ^ first)))
        pairs.append((2 * at + 1, 2 * (at ^ second) + 1))
    return lax.ppermute(x, ("seq", "chan"), pairs)


def local(latents, conv_in, conv_up, to_pixels, slot_anchor, slot_count):
    n = lax.axis_size("seq")
    current = latents[0]
    shard = current.shape[1]
    anchor = slot_anchor.transpose(1, 0, 2)
    in_flat = conv_in.reshape(-1, conv_in.shape[-1])
    pix = to_pixels.T
    routes = seq_routes(n)
    anchors = [spread(anchor, *route) for route in routes]
    tm_size = lax.axis_size("tm")
    previous = lax.ppermute(current, "tm", [(i, (i + 1) % tm_size) for i in range(tm_size)])
    other_in, other_up = swapped(in_flat), swapped(conv_up)
    padded = (shard - 1) // LANES * LANES + 2 * LANES
    own = (current, anchor, in_flat, pix, conv_up)
    cur_pad, anchor, own_in, own_pix, own_up = pl.pallas_call(
        stage,
        out_shape=[
            jax.ShapeDtypeStruct((C_LAT, padded), BF16),
            *(jax.ShapeDtypeStruct(x.shape, x.dtype) for x in own[1:]),
        ],
        in_specs=[HBM] * 5,
        out_specs=[VMEM] * 5,
        scratch_shapes=[
            pltpu.VMEM(current.shape, BF16),
            pltpu.SemaphoreType.DMA((5,)),
        ],
        compiler_params=pltpu.CompilerParams(vmem_limit_bytes=8 << 20),
        cost_estimate=pl.CostEstimate(flops=1, bytes_accessed=1, transcendentals=0),
        name="stage",
    )(*map(in_hbm, own))
    plain = jax.ShapeDtypeStruct((ROOM, C_LAT, LANES), BF16)
    cut = []
    for targets, shape, name in (([anchor], plain, "cut_own"), (anchors, plain, "cut_windows")):
        cut += pl.pallas_call(
            functools.partial(cut_windows, n),
            out_shape=[shape] * len(targets),
            in_specs=[VMEM] * (len(targets) + 2),
            out_specs=[VMEM] * len(targets),
            scratch_shapes=[pltpu.VMEM((C_LAT, padded), BF16)],
            compiler_params=pltpu.CompilerParams(vmem_limit_bytes=4 << 20),
            cost_estimate=pl.CostEstimate(flops=1, bytes_accessed=1, transcendentals=0),
            name=name,
        )(*targets, cur_pad, previous)
    parts = [cut[0]]
    for message, route in zip(cut[1:], routes[:-1]):
        arrived = spread(message, *route)
        parts += [arrived, swapped(arrived)]
    parts.append(spread(cut[-1], *routes[-1]))
    pixels = pl.pallas_call(
        functools.partial(decode, n),
        out_shape=jax.ShapeDtypeStruct((1, 3, 1, MAXT, LANES), BF16),
        in_specs=[SMEM] + [VMEM] * (n + 7),
        out_specs=VMEM,
        scratch_shapes=[
            pltpu.VMEM((n,) + plain.shape, BF16),
        ]
        + [pltpu.VMEM((TAPS, (TH + 2) * MAXT * TW, C_MID), BF16)] * TAPS,
        compiler_params=pltpu.CompilerParams(vmem_limit_bytes=32 << 20),
        name="decode",
    )(slot_count, anchor, *parts, own_in, other_in, own_pix, swapped(pix), own_up, other_up)
    return pixels.transpose(0, 3, 1, 2, 4)


def solution(mesh):
    placed = (
        P(("clip", "tm"), None, "seq"),
        P(None, None, None, None, "chan"),
        P(None, None, None, None, "chan"),
        P("chan", None),
        P(("clip", "tm"), None, "seq"),
        P(("clip", "tm"), "seq"),
    )
    return jax.shard_map(
        local,
        mesh=mesh,
        in_specs=placed,
        out_specs=P(("clip", "tm"), "seq", None, None, None),
        check_vma=False,
    )
```

```python
import functools

import jax
import jax.numpy as jnp
from jax import lax
from jax.experimental import pallas as pl
from jax.experimental.pallas import tpu as pltpu
from jax.sharding import PartitionSpec as P

H_LAT = 45
W_LAT = 160
C_LAT = 16
C_MID = 512
FG = 4
TH = 2
TW = 16
MAXT = 4
ROWS = TH + 4
COLS = TW + 4
LANES = 128
TAPS = 3
WIDE = 24
ROOM = 2 * MAXT
BF16 = jnp.bfloat16
F32 = jnp.float32
VMEM = pl.BlockSpec(memory_space=pltpu.VMEM)
SMEM = pl.BlockSpec(memory_space=pltpu.SMEM)
HBM = pl.BlockSpec(memory_space=pltpu.HBM)
ANY = pl.BlockSpec(memory_space=pl.ANY)


def lane_ids(rows):
    return lax.broadcasted_iota(jnp.int32, (rows, LANES), 1)


def silu(v):
    return v * (0.5 * jnp.tanh(0.5 * v) + 0.5)


def fetched(sources, targets, sems):
    copies = [pltpu.make_async_copy(*pair, sems.at[i]) for i, pair in enumerate(zip(sources, targets))]
    for copy in copies:
        copy.start()
    return copies


def stage(*refs):
    sources, (cur_out, *outs, cur, sems) = refs[:5], refs[5:]
    copies = []
    for i, pair in enumerate(zip(sources, (cur, *outs))):
        copies.append(pltpu.make_async_copy(*pair, sems.at[i]))
        copies[i].start()
    copies[0].wait()
    cur_out[:, : cur.shape[1]] = cur[...]
    for copy in copies[1:]:
        copy.wait()


def cut_windows(n, *refs):
    count = (len(refs) - 3) // 2
    anchors, (cur, prev_ref), outs, room = refs[:count], refs[count : count + 2], refs[count + 2 : -1], refs[-1]
    shard = prev_ref.shape[1]
    per_frame = n // FG
    part_start = lax.rem(lax.axis_index("seq"), per_frame) * shard
    last_base = (shard - 1) // LANES * LANES
    last_base = (shard - 1) // LANES * LANES
    lane = lane_ids(2 * C_LAT)
    spot_row, spot_col = lane // COLS, lane % COLS
    spot = jnp.where(spot_row < ROWS, spot_row * W_LAT + spot_col, -H_LAT * W_LAT)
    of_row = [spot_row == rho for rho in range(ROWS)]
    real = lax.axis_index("tm") > 0
    room[:C_LAT, :shard] = jnp.where(real, prev_ref[...], jnp.zeros((), BF16))
    room[C_LAT:, :shard] = cur[:, :shard]
    for k in range(count):
        anchor = anchors[k][...]
        for i in range(MAXT):
            col0 = anchor[2, 0, i] - 2
            origin = (anchor[1, 0, i] - 2) * W_LAT + col0 - part_start
            token, col = spot + origin, spot_col + col0
            keep = (token >= 0) & (token < shard) & (col >= 0) & (col < W_LAT)
            total = None
            for rho in range(ROWS):
                start = origin + rho * W_LAT
                base = jnp.minimum(jnp.maximum(start & -LANES, 0), last_base)
                base = pl.multiple_of(base, LANES)
                off = start - base
                both = room[:, pl.ds(base, 2 * LANES)]
                both = jnp.where(lane >= off, both[:, :LANES], both[:, LANES:])
                moved = pltpu.roll(both, (COLS * rho - off) & (LANES - 1), 1)
                total = moved if rho == 0 else jnp.where(of_row[rho], moved, total)
            total = jnp.where(keep, total, jnp.zeros((), BF16))
            for half in range(2):
                outs[k][half * MAXT + i] = total[half * C_LAT : (half + 1) * C_LAT]


def decode(n, *refs):
    count, anchor, parts = refs[0], refs[1][...], refs[2 : n + 2]
    own_in, other_in, own_pix, other_pix, own_up, other_up, out, held, *lineds = refs[n + 2 :]
    per_frame = n // FG
    me = lax.axis_index("seq")
    core = lax.axis_index("chan")
    held[me] = parts[0][...]
    routes = seq_routes(n)
    for k, (first, second) in enumerate(routes[:-1]):
        held[me ^ (first + core * (second - first))] = parts[2 * k + 1][...]
        held[me ^ (second + core * (first - second))] = parts[2 * k + 2][...]
    held[me ^ routes[-1][0]] = parts[n - 1][...]
    lane = lane_ids(C_LAT)

    firsts = [anchor[0, 0, i] & (FG - 1) for i in range(MAXT)]

    def frame(j):
        pieces = []
        for i in range(MAXT):
            at = firsts[i] + j
            late, rank = at >> 2, (at & (FG - 1)) * per_frame
            piece = held[rank, late * MAXT + i]
            for p in range(1, per_frame):
                piece += held[rank + p, late * MAXT + i]
            pieces.append(piece)
        result = []
        for rho in range(ROWS):
            total = None
            for i, piece in enumerate(pieces):
                by = (WIDE * i - COLS * rho) % LANES
                piece = pltpu.roll(piece, by, 1) if by else piece
                total = piece if i == 0 else jnp.where(lane >= WIDE * i, piece, total)
            result.append([total] + [pltpu.roll(total, LANES - c, 1) for c in range(1, TAPS)])
        return result

    def turned(pieces):
        zeros = [jnp.zeros((C_LAT, LANES), BF16)] * (LANES // C_LAT - len(pieces))
        return jnp.concatenate(pieces + zeros, axis=0).T[: MAXT * WIDE]

    taps = [(b, c) for b in range(TAPS) for c in range(TAPS)]
    spots = range(TH + 2)
    frames = [frame(j) for j in range(TAPS + 2)]
    cells = [
        jnp.concatenate([turned([frames[j][r + b][c] for b, c in taps[:-1]]) for r in spots], axis=0)
        for j in range(TAPS + 2)
    ]
    tail = jnp.concatenate([turned([frames[j][r + 2][2] for j in range(TAPS + 2)]) for r in spots], axis=0)
    x = lax.broadcasted_iota(jnp.int32, (WIDE, LANES), 0)
    quarter, half = C_MID // 4, C_MID // 2
    for t in range(TAPS):
        volume = jnp.concatenate([*cells[t : t + TAPS], tail], axis=1)
        lined = lineds[t]
        for first, weights in enumerate((own_in, other_in)):
            per_tap = len(taps) * C_LAT
            kernel = [weights[a * per_tap : a * per_tap + LANES] for a in range(TAPS)]
            for j in range(LANES // C_LAT):
                a = j - t
                ends = weights[a * per_tap + LANES : (a + 1) * per_tap] if 0 <= a < TAPS else None
                kernel.append(jnp.zeros((C_LAT, half), BF16) if ends is None else ends)
            pre = jnp.dot(volume, jnp.concatenate(kernel, axis=0), preferred_element_type=F32)
            for r in spots:
                for i in range(MAXT):
                    row = anchor[1, 0, i] - 1 + r
                    col = anchor[2, 0, i] - 1 + x
                    width = jnp.where((row >= 0) & (row < H_LAT), W_LAT, 0)
                    at = (r * MAXT + i) * WIDE
                    value = silu(pre[at : at + WIDE])
                    for q in range(2):
                        part = slice((2 * first + q) * quarter, (2 * first + q + 1) * quarter)
                        kept = jnp.where((col >= 0) & (col < width), value[:, q * quarter : (q + 1) * quarter], 0.0)
                        for c in range(TAPS):
                            moved = pltpu.roll(kept, WIDE - c, 0) if c else kept
                            lined[c, (r * MAXT + i) * TW : (r * MAXT + i + 1) * TW, part] = moved[:TW].astype(BF16)
    outs = own_up.shape[-1]
    span = MAXT * TW
    total = jnp.zeros((TH * span, 2 * outs), F32)
    for a in range(TAPS):
        for c in range(TAPS):
            for b in range(TAPS):
                rows = lineds[a][c, b * span : (b + TH) * span]
                for first in range(2):
                    here = pl.ds(pl.multiple_of((first ^ core) * half, half), half)
                    weights = jnp.concatenate([own_up[a, b, c, here], other_up[a, b, c, here]], axis=1)
                    total += jnp.dot(rows[:, first * half : (first + 1) * half], weights, preferred_element_type=F32)
    upper = silu(total).astype(BF16)
    row = lax.broadcasted_iota(jnp.int32, (32, 12), 0)
    col = lax.broadcasted_iota(jnp.int32, (32, 12), 1)
    pick = ((row % 8) * 4 + row // 8 == col) & (row % 8 < 3)
    pix = jnp.concatenate([own_pix[...], other_pix[...]], axis=1)
    pix = jnp.dot(pick.astype(BF16), pix, preferred_element_type=F32).astype(BF16)
    colors = lax.dot_general(pix, upper, (((1,), (1,)), ((), ())), preferred_element_type=F32)
    colors = colors.astype(BF16).astype(F32)
    lane = lane_ids(8)
    p, q = (lane // 32) % 2, lane % 2
    for i in range(MAXT):
        source = (lane // 64) * span + i * TW + (lane % 32) // 2
        pixel = jnp.zeros((8, LANES), F32)
        for pq in range(4):
            found = jnp.take_along_axis(colors[8 * pq : 8 * pq + 8], source, axis=1)
            pixel = jnp.where(2 * p + q == pq, found, pixel)
        pixel = jnp.where(i < count[0, 0], pixel, 0.0).astype(BF16)
        for e in range(3):
            out[0, e, 0, i : i + 1] = pixel[e : e + 1]


def in_hbm(x):
    return pltpu.with_memory_space_constraint(x, pltpu.HBM)


def seq_routes(n):
    codes = [1, *range(3, n), 2]
    return list(zip(codes[:-1:2], codes[1:-1:2])) + [(codes[-1], codes[-1])]


def swapped(x):
    return lax.ppermute(x, "chan", [(0, 1), (1, 0)])


def spread(x, first, second):
    pairs = []
    for at in range(lax.axis_size("seq")):
        pairs.append((2 * at, 2 * (at ^ first)))
        pairs.append((2 * at + 1, 2 * (at ^ second) + 1))
    return lax.ppermute(x, ("seq", "chan"), pairs)


def local(latents, conv_in, conv_up, to_pixels, slot_anchor, slot_count):
    n = lax.axis_size("seq")
    current = latents[0]
    shard = current.shape[1]
    anchor = slot_anchor.transpose(1, 0, 2)
    in_flat = conv_in.reshape(-1, conv_in.shape[-1])
    pix = to_pixels.T
    routes = seq_routes(n)
    anchors = [spread(anchor, *route) for route in routes]
    tm_size = lax.axis_size("tm")
    previous = lax.ppermute(current, "tm", [(i, (i + 1) % tm_size) for i in range(tm_size)])
    other_in, other_up = swapped(in_flat), swapped(conv_up)
    padded = (shard - 1) // LANES * LANES + 2 * LANES
    own = (current, anchor, in_flat, pix, conv_up)
    cur_pad, anchor, own_in, own_pix, own_up = pl.pallas_call(
        stage,
        out_shape=[
            jax.ShapeDtypeStruct((C_LAT, padded), BF16),
            *(jax.ShapeDtypeStruct(x.shape, x.dtype) for x in own[1:]),
        ],
        in_specs=[HBM] * 5,
        out_specs=[VMEM] * 5,
        scratch_shapes=[
            pltpu.VMEM(current.shape, BF16),
            pltpu.SemaphoreType.DMA((5,)),
        ],
        compiler_params=pltpu.CompilerParams(vmem_limit_bytes=8 << 20),
        cost_estimate=pl.CostEstimate(flops=1, bytes_accessed=1, transcendentals=0),
        name="stage",
    )(*map(in_hbm, own))
    plain = jax.ShapeDtypeStruct((ROOM, C_LAT, LANES), BF16)
    cut = []
    for targets, shape, name in (([anchor], plain, "cut_own"), (anchors, plain, "cut_windows")):
        cut += pl.pallas_call(
            functools.partial(cut_windows, n),
            out_shape=[shape] * len(targets),
            in_specs=[VMEM] * (len(targets) + 2),
            out_specs=[VMEM] * len(targets),
            scratch_shapes=[pltpu.VMEM((2 * C_LAT, padded), BF16)],
            compiler_params=pltpu.CompilerParams(vmem_limit_bytes=4 << 20),
            cost_estimate=pl.CostEstimate(flops=1, bytes_accessed=1, transcendentals=0),
            name=name,
        )(*targets, cur_pad, previous)
    parts = [cut[0]]
    for message, route in zip(cut[1:], routes[:-1]):
        arrived = spread(message, *route)
        parts += [arrived, swapped(arrived)]
    parts.append(spread(cut[-1], *routes[-1]))
    pixels = pl.pallas_call(
        functools.partial(decode, n),
        out_shape=jax.ShapeDtypeStruct((1, 3, 1, MAXT, LANES), BF16),
        in_specs=[SMEM] + [VMEM] * (n + 7),
        out_specs=VMEM,
        scratch_shapes=[
            pltpu.VMEM((n,) + plain.shape, BF16),
        ]
        + [pltpu.VMEM((TAPS, (TH + 2) * MAXT * TW, C_MID), BF16)] * TAPS,
        compiler_params=pltpu.CompilerParams(vmem_limit_bytes=32 << 20),
        name="decode",
    )(slot_count, anchor, *parts, own_in, other_in, own_pix, swapped(pix), own_up, other_up)
    return pixels.transpose(0, 3, 1, 2, 4)


def solution(mesh):
    placed = (
        P(("clip", "tm"), None, "seq"),
        P(None, None, None, None, "chan"),
        P(None, None, None, None, "chan"),
        P("chan", None),
        P(("clip", "tm"), None, "seq"),
        P(("clip", "tm"), "seq"),
    )
    return jax.shard_map(
        local,
        mesh=mesh,
        in_specs=placed,
        out_specs=P(("clip", "tm"), "seq", None, None, None),
        check_vma=False,
    )
```

```python
import functools

import jax
import jax.numpy as jnp
from jax import lax
from jax.experimental import pallas as pl
from jax.experimental.pallas import tpu as pltpu
from jax.sharding import PartitionSpec as P

H_LAT = 45
W_LAT = 160
C_LAT = 16
C_MID = 512
FG = 4
TH = 2
TW = 16
MAXT = 4
ROWS = TH + 4
COLS = TW + 4
LANES = 128
TAPS = 3
WIDE = 24
ROOM = 2 * MAXT
BF16 = jnp.bfloat16
F32 = jnp.float32
VMEM = pl.BlockSpec(memory_space=pltpu.VMEM)
SMEM = pl.BlockSpec(memory_space=pltpu.SMEM)
HBM = pl.BlockSpec(memory_space=pltpu.HBM)
ANY = pl.BlockSpec(memory_space=pl.ANY)


def lane_ids(rows):
    return lax.broadcasted_iota(jnp.int32, (rows, LANES), 1)


def silu(v):
    return v * (0.5 * jnp.tanh(0.5 * v) + 0.5)


def fetched(sources, targets, sems):
    copies = [pltpu.make_async_copy(*pair, sems.at[i]) for i, pair in enumerate(zip(sources, targets))]
    for copy in copies:
        copy.start()
    return copies


def stage(*refs):
    sources, (cur_out, *outs, cur, sems) = refs[:5], refs[5:]
    copies = []
    for i, pair in enumerate(zip(sources, (cur, *outs))):
        copies.append(pltpu.make_async_copy(*pair, sems.at[i]))
        copies[i].start()
    copies[0].wait()
    cur_out[:, : cur.shape[1]] = cur[...]
    for copy in copies[1:]:
        copy.wait()


def cut_windows(n, *refs):
    count = (len(refs) - 3) // 2
    anchors, (cur, prev_ref), outs, room = refs[:count], refs[count : count + 2], refs[count + 2 : -1], refs[-1]
    shard = prev_ref.shape[1]
    per_frame = n // FG
    part_start = lax.rem(lax.axis_index("seq"), per_frame) * shard
    last_base = (shard - 1) // LANES * LANES
    last_base = (shard - 1) // LANES * LANES
    lane = lane_ids(2 * C_LAT)
    spot_row, spot_col = lane // COLS, lane % COLS
    spot = jnp.where(spot_row < ROWS, spot_row * W_LAT + spot_col, -H_LAT * W_LAT)
    of_row = [spot_row == rho for rho in range(ROWS)]
    real = lax.axis_index("tm") > 0
    room[:C_LAT, :shard] = jnp.where(real, prev_ref[...], jnp.zeros((), BF16))
    room[C_LAT:, :shard] = cur[:, :shard]
    for k in range(count):
        anchor = anchors[k][...]
        for i in range(MAXT):
            col0 = anchor[2, 0, i] - 2
            origin = (anchor[1, 0, i] - 2) * W_LAT + col0 - part_start
            token, col = spot + origin, spot_col + col0
            keep = (token >= 0) & (token < shard) & (col >= 0) & (col < W_LAT)
            total = None
            for rho in range(ROWS):
                start = origin + rho * W_LAT
                base = jnp.minimum(jnp.maximum(start & -LANES, 0), last_base)
                base = pl.multiple_of(base, LANES)
                off = start - base
                both = room[:, pl.ds(base, 2 * LANES)]
                both = jnp.where(lane >= off, both[:, :LANES], both[:, LANES:])
                moved = pltpu.roll(both, (COLS * rho - off) & (LANES - 1), 1)
                total = moved if rho == 0 else jnp.where(of_row[rho], moved, total)
            total = jnp.where(keep, total, jnp.zeros((), BF16))
            for half in range(2):
                outs[k][half * MAXT + i] = total[half * C_LAT : (half + 1) * C_LAT]


def decode(n, *refs):
    count, anchor, parts = refs[0], refs[1][...], refs[2 : n + 2]
    own_in, other_in, own_pix, other_pix, own_up, other_up, out, held, *lineds = refs[n + 2 :]
    per_frame = n // FG
    me = lax.axis_index("seq")
    core = lax.axis_index("chan")
    held[me] = parts[0][...]
    routes = seq_routes(n)
    for k, (first, second) in enumerate(routes[:-1]):
        held[me ^ (first + core * (second - first))] = parts[2 * k + 1][...]
        held[me ^ (second + core * (first - second))] = parts[2 * k + 2][...]
    held[me ^ routes[-1][0]] = parts[n - 1][...]
    lane = lane_ids(C_LAT)

    firsts = [anchor[0, 0, i] & (FG - 1) for i in range(MAXT)]

    def frame(j):
        pieces = []
        for i in range(MAXT):
            at = firsts[i] + j
            late, rank = at >> 2, (at & (FG - 1)) * per_frame
            piece = held[rank, late * MAXT + i]
            for p in range(1, per_frame):
                piece += held[rank + p, late * MAXT + i]
            pieces.append(piece)
        result = []
        for rho in range(ROWS):
            total = None
            for i, piece in enumerate(pieces):
                by = (WIDE * i - COLS * rho) % LANES
                piece = pltpu.roll(piece, by, 1) if by else piece
                total = piece if i == 0 else jnp.where(lane >= WIDE * i, piece, total)
            result.append([total] + [pltpu.roll(total, LANES - c, 1) for c in range(1, TAPS)])
        return result

    def turned(pieces):
        zeros = [jnp.zeros((C_LAT, LANES), BF16)] * (LANES // C_LAT - len(pieces))
        return jnp.concatenate(pieces + zeros, axis=0).T[: MAXT * WIDE]

    taps = [(b, c) for b in range(TAPS) for c in range(TAPS)]
    spots = range(TH + 2)
    frames = [frame(j) for j in range(TAPS + 2)]
    cells = [
        jnp.concatenate([turned([frames[j][r + b][c] for b, c in taps[:-1]]) for r in spots], axis=0)
        for j in range(TAPS + 2)
    ]
    tail = jnp.concatenate([turned([frames[j][r + 2][2] for j in range(TAPS + 2)]) for r in spots], axis=0)
    x = lax.broadcasted_iota(jnp.int32, (WIDE, LANES), 0)
    quarter, half = C_MID // 4, C_MID // 2
    for t in range(TAPS):
        volume = jnp.concatenate([*cells[t : t + TAPS], tail[:, : (TAPS + 2) * C_LAT]], axis=1)
        lined = lineds[t]
        for first, weights in enumerate((own_in, other_in)):
            per_tap = len(taps) * C_LAT
            kernel = [weights[a * per_tap : a * per_tap + LANES] for a in range(TAPS)]
            for j in range(TAPS + 2):
                a = j - t
                ends = weights[a * per_tap + LANES : (a + 1) * per_tap] if 0 <= a < TAPS else None
                kernel.append(jnp.zeros((C_LAT, half), BF16) if ends is None else ends)
            pre = jnp.dot(volume, jnp.concatenate(kernel, axis=0), preferred_element_type=F32)
            for r in spots:
                for i in range(MAXT):
                    row = anchor[1, 0, i] - 1 + r
                    col = anchor[2, 0, i] - 1 + x
                    width = jnp.where((row >= 0) & (row < H_LAT), W_LAT, 0)
                    at = (r * MAXT + i) * WIDE
                    value = silu(pre[at : at + WIDE])
                    for q in range(2):
                        part = slice((2 * first + q) * quarter, (2 * first + q + 1) * quarter)
                        kept = jnp.where((col >= 0) & (col < width), value[:, q * quarter : (q + 1) * quarter], 0.0)
                        for c in range(TAPS):
                            moved = pltpu.roll(kept, WIDE - c, 0) if c else kept
                            lined[c, (r * MAXT + i) * TW : (r * MAXT + i + 1) * TW, part] = moved[:TW].astype(BF16)
    outs = own_up.shape[-1]
    span = MAXT * TW
    total = jnp.zeros((TH * span, 2 * outs), F32)
    for a in range(TAPS):
        for c in range(TAPS):
            for b in range(TAPS):
                rows = lineds[a][c, b * span : (b + TH) * span]
                for first in range(2):
                    here = pl.ds(pl.multiple_of((first ^ core) * half, half), half)
                    weights = jnp.concatenate([own_up[a, b, c, here], other_up[a, b, c, here]], axis=1)
                    total += jnp.dot(rows[:, first * half : (first + 1) * half], weights, preferred_element_type=F32)
    upper = silu(total).astype(BF16)
    row = lax.broadcasted_iota(jnp.int32, (32, 12), 0)
    col = lax.broadcasted_iota(jnp.int32, (32, 12), 1)
    pick = ((row % 8) * 4 + row // 8 == col) & (row % 8 < 3)
    pix = jnp.concatenate([own_pix[...], other_pix[...]], axis=1)
    pix = jnp.dot(pick.astype(BF16), pix, preferred_element_type=F32).astype(BF16)
    colors = lax.dot_general(pix, upper, (((1,), (1,)), ((), ())), preferred_element_type=F32)
    colors = colors.astype(BF16).astype(F32)
    lane = lane_ids(8)
    p, q = (lane // 32) % 2, lane % 2
    for i in range(MAXT):
        source = (lane // 64) * span + i * TW + (lane % 32) // 2
        pixel = jnp.zeros((8, LANES), F32)
        for pq in range(4):
            found = jnp.take_along_axis(colors[8 * pq : 8 * pq + 8], source, axis=1)
            pixel = jnp.where(2 * p + q == pq, found, pixel)
        pixel = jnp.where(i < count[0, 0], pixel, 0.0).astype(BF16)
        for e in range(3):
            out[0, e, 0, i : i + 1] = pixel[e : e + 1]


def in_hbm(x):
    return pltpu.with_memory_space_constraint(x, pltpu.HBM)


def seq_routes(n):
    codes = [1, *range(3, n), 2]
    return list(zip(codes[:-1:2], codes[1:-1:2])) + [(codes[-1], codes[-1])]


def swapped(x):
    return lax.ppermute(x, "chan", [(0, 1), (1, 0)])


def spread(x, first, second):
    pairs = []
    for at in range(lax.axis_size("seq")):
        pairs.append((2 * at, 2 * (at ^ first)))
        pairs.append((2 * at + 1, 2 * (at ^ second) + 1))
    return lax.ppermute(x, ("seq", "chan"), pairs)


def local(latents, conv_in, conv_up, to_pixels, slot_anchor, slot_count):
    n = lax.axis_size("seq")
    current = latents[0]
    shard = current.shape[1]
    anchor = slot_anchor.transpose(1, 0, 2)
    in_flat = conv_in.reshape(-1, conv_in.shape[-1])
    pix = to_pixels.T
    routes = seq_routes(n)
    anchors = [spread(anchor, *route) for route in routes]
    tm_size = lax.axis_size("tm")
    previous = lax.ppermute(current, "tm", [(i, (i + 1) % tm_size) for i in range(tm_size)])
    other_in, other_up = swapped(in_flat), swapped(conv_up)
    padded = (shard - 1) // LANES * LANES + 2 * LANES
    own = (current, anchor, in_flat, pix, conv_up)
    cur_pad, anchor, own_in, own_pix, own_up = pl.pallas_call(
        stage,
        out_shape=[
            jax.ShapeDtypeStruct((C_LAT, padded), BF16),
            *(jax.ShapeDtypeStruct(x.shape, x.dtype) for x in own[1:]),
        ],
        in_specs=[HBM] * 5,
        out_specs=[VMEM] * 5,
        scratch_shapes=[
            pltpu.VMEM(current.shape, BF16),
            pltpu.SemaphoreType.DMA((5,)),
        ],
        compiler_params=pltpu.CompilerParams(vmem_limit_bytes=8 << 20),
        cost_estimate=pl.CostEstimate(flops=1, bytes_accessed=1, transcendentals=0),
        name="stage",
    )(*map(in_hbm, own))
    plain = jax.ShapeDtypeStruct((ROOM, C_LAT, LANES), BF16)
    cut = []
    for targets, shape, name in (([anchor], plain, "cut_own"), (anchors, plain, "cut_windows")):
        cut += pl.pallas_call(
            functools.partial(cut_windows, n),
            out_shape=[shape] * len(targets),
            in_specs=[VMEM] * (len(targets) + 2),
            out_specs=[VMEM] * len(targets),
            scratch_shapes=[pltpu.VMEM((2 * C_LAT, padded), BF16)],
            compiler_params=pltpu.CompilerParams(vmem_limit_bytes=4 << 20),
            cost_estimate=pl.CostEstimate(flops=1, bytes_accessed=1, transcendentals=0),
            name=name,
        )(*targets, cur_pad, previous)
    parts = [cut[0]]
    for message, route in zip(cut[1:], routes[:-1]):
        arrived = spread(message, *route)
        parts += [arrived, swapped(arrived)]
    parts.append(spread(cut[-1], *routes[-1]))
    pixels = pl.pallas_call(
        functools.partial(decode, n),
        out_shape=jax.ShapeDtypeStruct((1, 3, 1, MAXT, LANES), BF16),
        in_specs=[SMEM] + [VMEM] * (n + 7),
        out_specs=VMEM,
        scratch_shapes=[
            pltpu.VMEM((n,) + plain.shape, BF16),
        ]
        + [pltpu.VMEM((TAPS, (TH + 2) * MAXT * TW, C_MID), BF16)] * TAPS,
        compiler_params=pltpu.CompilerParams(vmem_limit_bytes=32 << 20),
        name="decode",
    )(slot_count, anchor, *parts, own_in, other_in, own_pix, swapped(pix), own_up, other_up)
    return pixels.transpose(0, 3, 1, 2, 4)


def solution(mesh):
    placed = (
        P(("clip", "tm"), None, "seq"),
        P(None, None, None, None, "chan"),
        P(None, None, None, None, "chan"),
        P("chan", None),
        P(("clip", "tm"), None, "seq"),
        P(("clip", "tm"), "seq"),
    )
    return jax.shard_map(
        local,
        mesh=mesh,
        in_specs=placed,
        out_specs=P(("clip", "tm"), "seq", None, None, None),
        check_vma=False,
    )
```
